32 devices in a mesh: elem: 32 (over z, y, x, core).
Axes of the slice: x: 2, y: 2, z: 4, core: 2. Of those that a mesh axis runs over, the one named last changes fastest.
Arguments:
- a_blocks: float32 [1024, 7, 4096], P('elem'), may hold values from -0.25 to 0.25
- p_blocks: float32 [1024, 2, 4096], P('elem'), may hold values from -1.2 to 1.2
- a_slot: int32 [1024, 7], P('elem'), may hold values from 0 to 93
- serve_rows: int32 [32, 31, 2], P('elem'), may hold values from 0 to 31
- row_count: int32 [32], P('elem'), may hold values from 8 to 32, as said below
- contrib_slot: int32 [1024, 28], P('elem'), may hold values from 0 to 127
- recv_tile: int32 [32, 32, 4], P('elem'), may hold values from 0 to 7
Outputs:
- coarse: float32 [256, 4096], P('elem')
The draws below stay inside these ranges and needn't reach their ends.
Inputs may be any that keep to these rules, and one draw needn't show every extreme that they name: `row_count`: rows of a device at or beyond its count are padding and contribute nothing; some device has exactly 32.
All inputs are finite; a program needn't handle non-finite values.
Results may differ from the reference program's by a relative error of at most 0.0003.
Values sent between devices are 32-bit elements; how exact they have to be, the bound alone decides.
No kernel may reach another device: no remote copies, remote signals or barrier semaphores. Data moves between devices by JAX's collectives and lax.ppermute only.
A program may use at most 192 MiB of HBM per device.

```python
import jax
import jax.numpy as jnp
from jax import lax

B = 64
KA = 7
KP = 2
S = 2
CAP = 4
TO = 8
R = 32
NB = 31
NO = 32
NF = 1024
N_ELEM = 32


def draw_row_count(key, part):
    first, second = jax.random.split(jax.random.fold_in(key, 17))
    counts = jax.random.randint(first, (N_ELEM,), R // 4, R + 1)
    chosen = jax.random.randint(second, (), 0, N_ELEM)
    return jnp.where(jnp.arange(N_ELEM) == chosen, R, counts).astype(jnp.int32)


def draw_a_slot(key, part):
    first, second, third = jax.random.split(jax.random.fold_in(key, 23), 3)
    pick = jax.random.randint(first, (NF, KA), 0, 2)
    own = jax.random.randint(second, (NF, KA), 0, R)
    far = jax.random.randint(third, (NF, KA), R, R + (N_ELEM - 1) * S)
    return jnp.where(pick == 0, own, far).astype(jnp.int32)


def draw_contrib_slot(key, part):
    first, second, third = jax.random.split(jax.random.fold_in(key, 29), 3)
    shape = (NF, KP * KA * KP)
    pick = jax.random.randint(first, shape, 0, 2)
    home = jax.random.randint(second, shape, 0, CAP)
    spread = jax.random.randint(third, shape, 0, N_ELEM * CAP)
    return jnp.where(pick == 0, home, spread).astype(jnp.int32)


def with_ends(drawn, stream_key, least, largest):
    shape = drawn.shape
    spot = [jax.random.randint(jax.random.fold_in(stream_key, axis), (), 0, shape[axis]) for axis in range(len(shape))]
    drawn = drawn.at[tuple(spot)].set(least)
    longest = shape.index(max(shape))
    spot[longest] = (spot[longest] + 1) % shape[longest]
    return drawn.at[tuple(spot)].set(largest)


def shard_levels(key, dims, cuts, low, high):
    def one(dim, parts):
        draws = jax.random.uniform(jax.random.fold_in(jax.random.fold_in(key, 6), dim), (parts,), jnp.float32, low / len(cuts), high / len(cuts))
        return jnp.repeat(jnp.exp(draws), dims[dim] // parts).reshape((-1,) + (1,) * (len(dims) - dim - 1))

    factor_of = one(*cuts[0])
    for cut in cuts[1:]:
        factor_of = factor_of * one(*cut)
    return factor_of


def bell_draw(rng, dims, scale, reach, cuts=(), kind=jnp.bfloat16):
    drawn = scale * jax.random.normal(rng, dims, jnp.float32)
    if cuts:
        drawn = drawn * shard_levels(rng, dims, cuts, -0.22, 0.18)
    return jnp.clip(drawn, -reach, reach).astype(kind)


def setup_inputs(seed: int = 0) -> dict:
    splits = jax.random.split(jax.random.key(seed), 8)
    return {
        "a_blocks": bell_draw(splits[0], (NF, KA, B * B), (B * KA) ** -0.5, 0.25, ((0, 32),), jnp.float32),
        "p_blocks": bell_draw(splits[1], (NF, KP, B * B), 0.15, 1.2, ((0, 32),), jnp.float32),
        "a_slot": draw_a_slot(jax.random.fold_in(splits[7], 71), 0),
        "serve_rows": with_ends(jax.random.randint(splits[3], (N_ELEM, NB, S), 0, R), jax.random.fold_in(splits[3], 1), 0, R - 1).astype(jnp.int32),
        "row_count": draw_row_count(jax.random.fold_in(splits[7], 71), 0),
        "contrib_slot": draw_contrib_slot(jax.random.fold_in(splits[7], 71), 0),
        "recv_tile": with_ends(jax.random.randint(splits[6], (N_ELEM, NO, CAP), 0, TO), jax.random.fold_in(splits[6], 1), 0, TO - 1).astype(jnp.int32),
    }


def reference(a_blocks, p_blocks, a_slot, serve_rows, row_count, contrib_slot, recv_tile):
    ndev = N_ELEM
    count_near = N_ELEM - 1
    count_all = N_ELEM
    a_four = a_blocks.reshape(ndev, R, KA, B, B)
    p_four = p_blocks.reshape(ndev, R, KP, B, B)
    p_flat = p_blocks.reshape(ndev * R, KP, B, B)
    slot_three = a_slot.reshape(ndev, R, KA)
    contrib = contrib_slot.reshape(ndev, R * KP * KA * KP)
    near = jnp.arange(count_near, dtype=jnp.int32) + 1
    every = jnp.arange(count_all, dtype=jnp.int32)
    positions = jnp.arange(count_near, dtype=jnp.int32)
    sources = jnp.arange(ndev, dtype=jnp.int32)
    slot_ids = jnp.arange(count_all * CAP, dtype=jnp.int32)
    which = slot_ids // CAP
    within = slot_ids % CAP
    local_rows = jnp.arange(R, dtype=jnp.int32)

    def one_device(total, device):
        servers = (device - near) % ndev
        row_ids = (servers[:, None] * R + serve_rows[servers, positions]).reshape(-1)
        fetched = p_flat[row_ids]
        own = p_four[device]
        extended = jnp.concatenate([own, fetched], axis=0)
        neigh = extended[slot_three[device]]
        product = jnp.einsum('ikxy,ikqyz->ikqxz', a_four[device], neigh, precision=lax.Precision.HIGHEST)
        part = jnp.einsum('ipyx,ikqyz->ipkqxz', own, product, precision=lax.Precision.HIGHEST)
        live = (local_rows < row_count[device]).astype(jnp.float32)
        part = part * live[:, None, None, None, None, None]
        slots = jax.ops.segment_sum(part.reshape(-1, B * B), contrib[device], num_segments=count_all * CAP)
        owners = (device + every[which]) % ndev
        target = owners * TO + recv_tile[owners, which, within]
        return total.at[target].add(slots), None

    coarse, _ = lax.scan(one_device, jnp.zeros((ndev * TO, B * B), jnp.float32), sources)
    return coarse
```

```python
import functools

import jax
import jax.numpy as jnp
from jax import lax
from jax.experimental import pallas as pl
from jax.experimental.pallas import tpu as pltpu
from jax.sharding import PartitionSpec as P

B = 64
HALF = B // 2
LANES = 2 * B
TO = 8
UNROLL = 4
RING = 16
META = 8
VMEM_LIMIT = 56 * 1024 * 1024


def low_lanes(rows):
    return lax.broadcasted_iota(jnp.int32, (rows, LANES), 1) < B


def split_rows(value):
    high = value.astype(jnp.bfloat16)
    low = (value - high.astype(jnp.float32)).astype(jnp.bfloat16)
    return jnp.concatenate([high, high, low, low], axis=0)


def params(**more):
    return pltpu.CompilerParams(vmem_limit_bytes=VMEM_LIMIT, **more)


def prep_kernel(n, serve_count, me_ref, serve_ref, p_ref, own_out, send_out, own, sems, own_sem):
    rows = p_ref.shape[0]
    mask = low_lanes(HALF)

    def relayout(i, carry):
        first = p_ref[i, pl.ds(0, HALF, stride=2), :]
        second = p_ref[i, pl.ds(1, HALF, stride=2), :]
        own[i, pl.ds(0, HALF, stride=2), :] = jnp.where(mask, first, pltpu.roll(second, B, 1))
        own[i, pl.ds(1, HALF, stride=2), :] = jnp.where(mask, pltpu.roll(first, B, 1), second)
        return carry

    lax.fori_loop(0, rows, relayout, 0, unroll=4)
    me = me_ref[0]
    own_copy = pltpu.make_async_copy(own, own_out, own_sem)

    def copy(target, c, row):
        return pltpu.make_async_copy(own.at[row], send_out.at[target, c], sems.at[target, c])

    def send(target, carry):
        offset = target - me - 1
        offset = jnp.where(offset < 0, offset + n, offset)
        offset = jnp.minimum(offset, n - 2)
        for c in range(serve_count):
            copy(target, c, serve_ref[0, offset, c]).start()
        return carry

    def finish(target, carry):
        for c in range(serve_count):
            copy(target, c, 0).wait()
        return carry

    lax.fori_loop(0, n, send, 0)
    own_copy.start()
    lax.fori_loop(0, n, finish, 0)
    own_copy.wait()


def add_products(acc, out, dest):
    mask = low_lanes(B)
    for p in range(2):
        rows = out[p * B : (p + 1) * B]
        left = jnp.where(mask, rows, 0.0)
        acc[dest[2 * p]] += left
        acc[dest[2 * p + 1]] += rows - left


def fold(acc, slot):
    even = acc[slot, pl.ds(0, HALF, stride=2), :]
    odd = acc[slot, pl.ds(1, HALF, stride=2), :]
    even = even + pltpu.roll(even, B, 1)
    odd = odd + pltpu.roll(odd, B, 1)
    return jnp.where(low_lanes(HALF), even, odd)


def near_kernel(n, count_row, a_slot, contrib, me_ref, own_ref, a_ref, left_ref, slots_ref, meta_ref, acc, near_meta):
    step = pl.program_id(0)
    rows = own_ref.shape[0]
    blocks = a_ref.shape[1]
    slot_count = slots_ref.shape[0]
    per_row = contrib.shape[1] // 2

    @pl.when(step == 0)
    def start():
        acc[...] = jnp.zeros_like(acc)

    mask = low_lanes(HALF)
    y_even = own_ref[step, pl.ds(0, HALF, stride=2), :]
    y_odd = own_ref[step, pl.ds(1, HALF, stride=2), :]
    p_rows = jnp.concatenate([y_even, y_odd], axis=0)
    high = p_rows.astype(jnp.bfloat16).astype(jnp.float32)
    pair = jnp.concatenate([high, p_rows - high], axis=0).T.astype(jnp.bfloat16)
    lhs = jnp.concatenate([pair, pair], axis=1)
    for k in range(blocks):
        tile = a_ref[0, k]
        turned = pltpu.roll(tile, B, 1)
        both = jnp.concatenate([jnp.where(mask, tile, turned), jnp.where(mask, turned, tile)], axis=0)
        left = jnp.dot(lhs, split_rows(both), preferred_element_type=jnp.float32)
        left_high = left.astype(jnp.bfloat16).astype(jnp.float32)
        packed = jnp.where(low_lanes(2 * B), left_high, left - left_high)
        left_ref[step * blocks + k] = packed.astype(jnp.bfloat16)

    @pl.when(step == pl.num_programs(0) - 1)
    def own_products():
        me = me_ref[0]
        live = count_row[0]

        def put(ref, at, f, row, i, k):
            ref[at * META] = f
            ref[at * META + 1] = row
            for p in range(2):
                for q in range(2):
                    ref[at * META + 2 + 2 * p + q] = contrib[i, p * per_row + 2 * k + q]

        def put_pad(ref, at):
            ref[at * META] = 0
            ref[at * META + 1] = 0
            for j in range(4):
                ref[at * META + 2 + j] = slot_count

        def scan_row(i, carry):
            near_count, far_count = carry
            for k in range(blocks):
                slot = a_slot[i, k]
                is_near = slot < rows
                index = slot - rows
                source = me - 1 - index // 2
                source = jnp.where(source < 0, source + n, source)
                f = i * blocks + k
                put(near_meta, near_count, f, jnp.where(is_near, slot, 0), i, k)
                put(meta_ref, far_count, f, jnp.where(is_near, 0, source * 2 + index % 2), i, k)
                near_count = near_count + jnp.where(is_near, 1, 0)
                far_count = far_count + jnp.where(is_near, 0, 1)
            return near_count, far_count

        near_count, far_count = lax.fori_loop(0, jnp.minimum(live, rows), scan_row, (0, 0))
        for j in range(UNROLL):
            put_pad(near_meta, near_count + j)
            put_pad(meta_ref, far_count + j)
        meta_ref[meta_ref.shape[0] - 1] = far_count

        def products(g, carry):
            for u in range(UNROLL):
                at = (g * UNROLL + u) * META
                lp = left_ref[near_meta[at]]
                weights = split_rows(own_ref[near_meta[at + 1]])
                out = jnp.dot(jnp.concatenate([lp, lp], axis=1), weights, preferred_element_type=jnp.float32)
                add_products(acc, out, [near_meta[at + 2 + j] for j in range(4)])
            return carry

        lax.fori_loop(0, (near_count + UNROLL - 1) // UNROLL, products, 0)

        def pack(slot, carry):
            slots_ref[slot] = fold(acc, slot)
            return carry

        lax.fori_loop(0, slot_count, pack, 0, unroll=2)


def far_kernel(n, cap, me_ref, meta, left_hbm, recv_hbm, near_hbm, send_hbm, acc, recv, near, packed, ring, ring_sems, sems, out_sems):
    me = me_ref[0]
    slot_count = near.shape[0]
    recv_copy = pltpu.make_async_copy(recv_hbm, recv, sems.at[0])
    near_copy = pltpu.make_async_copy(near_hbm, near, sems.at[1])
    recv_copy.start()
    count = meta[meta.shape[0] - 1]
    groups = (count + UNROLL - 1) // UNROLL
    depth = RING // UNROLL

    def left_copy(entry, buffer):
        return pltpu.make_async_copy(left_hbm.at[meta[entry * META]], ring.at[buffer], ring_sems.at[buffer])

    def fetch(g):
        @pl.when(g < groups)
        def go():
            for u in range(UNROLL):
                left_copy(g * UNROLL + u, lax.rem(g, depth) * UNROLL + u).start()

    for g in range(depth - 1):
        fetch(g)
    near_copy.start()
    acc[...] = jnp.zeros_like(acc)
    recv_copy.wait()

    def products(g, carry):
        fetch(g + depth - 1)
        for u in range(UNROLL):
            left_copy(0, lax.rem(g, depth) * UNROLL + u).wait()
        for u in range(UNROLL):
            at = (g * UNROLL + u) * META
            lp = ring[lax.rem(g, depth) * UNROLL + u]
            weights = split_rows(recv[meta[at + 1]])
            out = jnp.dot(jnp.concatenate([lp, lp], axis=1), weights, preferred_element_type=jnp.float32)
            add_products(acc, out, [meta[at + 2 + j] for j in range(4)])
        return carry

    lax.fori_loop(0, groups, products, 0)
    near_copy.wait()

    def out_copy(m):
        owner = me + m
        owner = jnp.where(owner >= n, owner - n, owner)
        return pltpu.make_async_copy(packed.at[m], send_hbm.at[owner], out_sems.at[m])

    def pack(m, carry):
        for c in range(cap):
            slot = m * cap + c
            packed[m, c] = fold(acc, slot) + near[slot]
        out_copy(m).start()
        return carry

    lax.fori_loop(0, n, pack, 0)

    def finish(m, carry):
        out_copy(m).wait()
        return carry

    lax.fori_loop(0, n, finish, 0)


def final_kernel(n, cap, me_ref, tile_ref, got_ref, out_ref, total):
    me = me_ref[0]
    total[...] = jnp.zeros_like(total)

    def add(source, carry):
        m = me - source
        m = jnp.where(m < 0, m + n, m)
        for c in range(cap):
            rows = pl.ds(pl.multiple_of(tile_ref[0, m, c] * HALF, HALF), HALF)
            total[rows, :] += got_ref[source, c]
        return carry

    lax.fori_loop(0, n, add, 0)
    for r in range(HALF):
        out_ref[:, r * LANES : (r + 1) * LANES] = total[pl.ds(r, TO, stride=HALF), :]


def spec(space):
    return pl.BlockSpec(memory_space=space)


def body(a_blocks, p_blocks, a_slot, serve_rows, row_count, contrib_slot, recv_tile):
    n = lax.axis_size("elem")
    rows, blocks, _ = a_blocks.shape
    cap = recv_tile.shape[2]
    serve_count = serve_rows.shape[2]
    f32, i32, bf16 = jnp.float32, jnp.int32, jnp.bfloat16
    smem, vmem, hbm = spec(pltpu.SMEM), spec(pltpu.VMEM), spec(pl.ANY)
    me = lax.axis_index("elem").astype(i32).reshape(1)
    shape = jax.ShapeDtypeStruct

    p_view = p_blocks.reshape(rows, 2, HALF, LANES).transpose(0, 2, 1, 3).reshape(rows, B, LANES)
    own, send = pl.pallas_call(
        functools.partial(prep_kernel, n, serve_count),
        out_shape=(shape((rows, B, LANES), f32), shape((n, serve_count, B, LANES), f32)),
        in_specs=[smem, smem, vmem],
        out_specs=(hbm, hbm),
        scratch_shapes=[
            pltpu.VMEM((rows, B, LANES), f32),
            pltpu.SemaphoreType.DMA((n, serve_count)),
            pltpu.SemaphoreType.DMA,
        ],
        compiler_params=params(),
        name="prep",
    )(me, serve_rows, p_view)

    recv = lax.all_to_all(
        send.reshape(n, serve_count * B, LANES), "elem", split_axis=0, concat_axis=0, tiled=True
    ).reshape(n * serve_count, B, LANES)

    entries = rows * blocks
    slot_count = n * cap
    meta_size = (entries + 2 * UNROLL) * META
    a_tiles = a_blocks.reshape(rows, blocks, HALF, LANES)
    left, near_slots, meta = pl.pallas_call(
        functools.partial(near_kernel, n),
        grid=(rows,),
        out_shape=(
            shape((entries, 2 * B, LANES), bf16),
            shape((slot_count, HALF, LANES), f32),
            shape((meta_size,), i32),
        ),
        in_specs=[
            smem,
            smem,
            smem,
            smem,
            pl.BlockSpec((rows, B, LANES), lambda i: (0, 0, 0)),
            pl.BlockSpec((1, blocks, HALF, LANES), lambda i: (i, 0, 0, 0)),
        ],
        out_specs=(
            pl.BlockSpec((entries, 2 * B, LANES), lambda i: (0, 0, 0)),
            pl.BlockSpec((slot_count, HALF, LANES), lambda i: (0, 0, 0)),
            smem,
        ),
        scratch_shapes=[pltpu.VMEM((slot_count + 1, B, LANES), f32), pltpu.SMEM((meta_size,), i32)],
        compiler_params=params(dimension_semantics=("arbitrary",)),
        cost_estimate=pl.CostEstimate(flops=8 * entries * 2 * B * LANES * LANES, bytes_accessed=16 << 20, transcendentals=0),
        name="near",
    )(row_count, a_slot, contrib_slot, me, own, a_tiles)

    send_two = pl.pallas_call(
        functools.partial(far_kernel, n, cap),
        out_shape=shape((n, cap, HALF, LANES), f32),
        in_specs=[smem, smem, hbm, hbm, hbm],
        out_specs=hbm,
        scratch_shapes=[
            pltpu.VMEM((slot_count + 1, B, LANES), f32),
            pltpu.VMEM((n * serve_count, B, LANES), f32),
            pltpu.VMEM((slot_count, HALF, LANES), f32),
            pltpu.VMEM((n, cap, HALF, LANES), f32),
            pltpu.VMEM((RING, 2 * B, LANES), bf16),
            pltpu.SemaphoreType.DMA((RING,)),
            pltpu.SemaphoreType.DMA((2,)),
            pltpu.SemaphoreType.DMA((n,)),
        ],
        compiler_params=params(),
        cost_estimate=pl.CostEstimate(flops=4 * entries * 2 * B * LANES * LANES, bytes_accessed=16 << 20, transcendentals=0),
        name="far",
    )(me, meta, left, recv, near_slots)

    got = lax.all_to_all(
        send_two.reshape(n, cap * HALF, LANES), "elem", split_axis=0, concat_axis=0, tiled=True
    ).reshape(n, cap, HALF, LANES)

    return pl.pallas_call(
        functools.partial(final_kernel, n, cap),
        out_shape=shape((TO, B * B), f32),
        in_specs=[smem, smem, vmem],
        out_specs=vmem,
        scratch_shapes=[pltpu.VMEM((TO * HALF, LANES), f32)],
        compiler_params=params(),
        name="final",
    )(me, recv_tile, got)


def solution(mesh):
    in_specs = (
        P("elem", None, None),
        P("elem", None, None),
        P("elem", None),
        P("elem", None, None),
        P("elem"),
        P("elem", None),
        P("elem", None, None),
    )
    out_specs = P("elem", None)
    return jax.shard_map(body, mesh=mesh, in_specs=in_specs, out_specs=out_specs, check_vma=False)
```

```python
import functools

import jax
import jax.numpy as jnp
from jax import lax
from jax.experimental import pallas as pl
from jax.experimental.pallas import tpu as pltpu
from jax.sharding import PartitionSpec as P

B = 64
HALF = B // 2
LANES = 2 * B
TO = 8
PLACES = 4
GROUP = 2 * PLACES
CHUNKS = 4
RING = 16
UNROLL = 4
META = 8
MIB = 1 << 20


def low_lanes(rows):
    return lax.broadcasted_iota(jnp.int32, (rows, LANES), 1) < B


def split_rows(value):
    high = value.astype(jnp.bfloat16)
    low = (value - high.astype(jnp.float32)).astype(jnp.bfloat16)
    return jnp.concatenate([high, high, low, low], axis=0)


def params(mib, **more):
    return pltpu.CompilerParams(vmem_limit_bytes=mib * MIB, **more)


def prep_kernel(n, me_ref, serve_hbm, p_hbm, own, send_hbm, p_ref, serve_ref, p_sems, serve_sem, send_sem):
    rows = p_ref.shape[0]
    serve_count = serve_ref.shape[0]
    mask = low_lanes(HALF)
    chunk = rows // CHUNKS

    def chunk_copy(i):
        part = pl.ds(i * chunk, chunk)
        return pltpu.make_async_copy(p_hbm.at[part], p_ref.at[part], p_sems.at[i])

    serve_copy = pltpu.make_async_copy(serve_hbm, serve_ref, serve_sem)
    for i in range(CHUNKS):
        chunk_copy(i).start()
    serve_copy.start()

    def relayout(i, carry):
        first = p_ref[i, pl.ds(0, HALF, stride=2), :]
        second = p_ref[i, pl.ds(1, HALF, stride=2), :]
        turned = pltpu.roll(jnp.where(mask, second, first), B, 1)
        own[i, pl.ds(0, HALF, stride=2), :] = jnp.where(mask, first, turned)
        own[i, pl.ds(1, HALF, stride=2), :] = jnp.where(mask, turned, second)
        return carry

    for i in range(CHUNKS):
        chunk_copy(i).wait()
        lax.fori_loop(i * chunk, (i + 1) * chunk, relayout, 0, unroll=4)
    serve_copy.wait()
    me = me_ref[0]

    def serve(target, carry):
        offset = target - me - 1
        offset = jnp.where(offset < 0, offset + n, offset)
        offset = jnp.minimum(offset, n - 2)
        for c in range(serve_count):
            pltpu.make_async_copy(own.at[serve_ref[c, offset]], send_hbm.at[target, c], send_sem).start()
        return carry

    lax.fori_loop(0, n, serve, 0, unroll=4)
    pltpu.make_async_copy(send_hbm, send_hbm, send_sem).wait()


def add_products(acc, out, dest):
    mask = low_lanes(B)
    for p in range(2):
        rows = out[p * B : (p + 1) * B]
        left = jnp.where(mask, rows, 0.0)
        acc[dest[2 * p]] += left
        acc[dest[2 * p + 1]] += rows - left


def fold(acc, slot):
    mask = low_lanes(HALF)
    even = acc[slot, pl.ds(0, HALF, stride=2), :]
    odd = acc[slot, pl.ds(1, HALF, stride=2), :]
    return jnp.where(mask, even, odd) + pltpu.roll(jnp.where(mask, odd, even), B, 1)


def near_kernel(
    n, count_row, a_slot, contrib, me_ref, own_ref, a_ref, left_hbm, slots_hbm, meta_ref, acc, left_ref, slots_ref, near_meta, sems
):
    step = pl.program_id(0)
    rows = own_ref.shape[0]
    blocks = a_ref.shape[1]
    slot_count = slots_ref.shape[0]
    per_row = contrib.shape[1] // 2

    @pl.when(step == 0)
    def start():
        acc[...] = jnp.zeros_like(acc)

    mask = low_lanes(HALF)
    y_even = own_ref[step, pl.ds(0, HALF, stride=2), :]
    y_odd = own_ref[step, pl.ds(1, HALF, stride=2), :]
    p_rows = jnp.concatenate([y_even, y_odd], axis=0)
    high = p_rows.astype(jnp.bfloat16).astype(jnp.float32)
    pair = jnp.concatenate([high, p_rows - high], axis=0).T.astype(jnp.bfloat16)
    lhs = jnp.concatenate([pair, pair], axis=1)
    for k in range(blocks):
        tile = a_ref[0, k]
        turned = pltpu.roll(tile, B, 1)
        both = jnp.concatenate([jnp.where(mask, tile, turned), jnp.where(mask, turned, tile)], axis=0)
        left = jnp.dot(lhs, split_rows(both), preferred_element_type=jnp.float32)
        left_high = left.astype(jnp.bfloat16).astype(jnp.float32)
        packed = jnp.where(low_lanes(2 * B), left_high, left - left_high)
        left_ref[step * blocks + k] = packed.astype(jnp.bfloat16)
    part = pl.ds(step * blocks, blocks)
    pltpu.make_async_copy(left_ref.at[part], left_hbm.at[part], sems.at[0]).start()

    @pl.when(step == pl.num_programs(0) - 1)
    def own_products():
        me = me_ref[0]
        live = count_row[0]

        def put(ref, at, f, row, i, k):
            ref[at * META] = f
            ref[at * META + 1] = row
            for p in range(2):
                for q in range(2):
                    ref[at * META + 2 + 2 * p + q] = contrib[i, p * per_row + 2 * k + q]

        def put_pad(ref, at):
            ref[at * META] = 0
            ref[at * META + 1] = 0
            for j in range(4):
                ref[at * META + 2 + j] = slot_count

        def scan_row(i, carry):
            near_count, far_count = carry
            for k in range(blocks):
                slot = a_slot[k, i]
                is_near = slot < rows
                index = slot - rows
                source = me - 1 - index // 2
                source = jnp.where(source < 0, source + n, source)
                f = i * blocks + k
                put(near_meta, near_count, f, jnp.where(is_near, slot, 0), i, k)
                put(meta_ref, far_count, f, jnp.where(is_near, 0, source * 2 + index % 2), i, k)
                near_count = near_count + jnp.where(is_near, 1, 0)
                far_count = far_count + jnp.where(is_near, 0, 1)
            return near_count, far_count

        near_count, far_count = lax.fori_loop(0, jnp.minimum(live, rows), scan_row, (0, 0))
        for j in range(UNROLL):
            put_pad(near_meta, near_count + j)
            put_pad(meta_ref, far_count + j)
        meta_ref[meta_ref.shape[0] - 1] = far_count

        def products(g, carry):
            for u in range(UNROLL):
                at = (g * UNROLL + u) * META
                lp = left_ref[near_meta[at]]
                weights = split_rows(own_ref[near_meta[at + 1]])
                out = jnp.dot(jnp.concatenate([lp, lp], axis=1), weights, preferred_element_type=jnp.float32)
                add_products(acc, out, [near_meta[at + 2 + j] for j in range(4)])
            return carry

        lax.fori_loop(0, (near_count + UNROLL - 1) // UNROLL, products, 0)

        def pack(slot, carry):
            slots_ref[slot] = fold(acc, slot)
            return carry

        lax.fori_loop(0, slot_count, pack, 0, unroll=2)
        slots_copy = pltpu.make_async_copy(slots_ref, slots_hbm, sems.at[1])
        slots_copy.start()
        pltpu.make_async_copy(left_hbm, left_hbm, sems.at[0]).wait()
        slots_copy.wait()


def far_kernel(n, cap, me_ref, meta, left_hbm, recv, near_hbm, *refs):
    far_slots, own_slots = refs[:PLACES], refs[PLACES : 2 * PLACES]
    acc, near, ring, ring_sems, near_sem = refs[2 * PLACES :]
    me = me_ref[0]
    count = meta[meta.shape[0] - 1]
    turns = (count + UNROLL - 1) // UNROLL
    depth = RING // UNROLL

    def fetch(g):
        @pl.when(g < turns)
        def go():
            for u in range(UNROLL):
                buffer = lax.rem(g, depth) * UNROLL + u
                source = left_hbm.at[meta[(g * UNROLL + u) * META]]
                pltpu.make_async_copy(source, ring.at[buffer], ring_sems.at[buffer]).start()

    for g in range(depth - 1):
        fetch(g)
    near_copy = pltpu.make_async_copy(near_hbm, near, near_sem)
    near_copy.start()
    acc[...] = jnp.zeros_like(acc)

    def products(g, carry):
        fetch(g + depth - 1)
        for u in range(UNROLL):
            buffer = lax.rem(g, depth) * UNROLL + u
            pltpu.make_async_copy(left_hbm.at[0], ring.at[buffer], ring_sems.at[buffer]).wait()
        for u in range(UNROLL):
            at = (g * UNROLL + u) * META
            lp = ring[lax.rem(g, depth) * UNROLL + u]
            weights = split_rows(recv[meta[at + 1]])
            out = jnp.dot(jnp.concatenate([lp, lp], axis=1), weights, preferred_element_type=jnp.float32)
            add_products(acc, out, [meta[at + 2 + j] for j in range(4)])
        return carry

    lax.fori_loop(0, turns, products, 0)
    near_copy.wait()
    groups = n // GROUP
    place = lax.rem(me // 2, PLACES)
    group = me // GROUP

    def pack(j, step, target):
        at = group + step
        at = jnp.where(at >= groups, at - groups, at)
        for core in range(2):
            m = at * GROUP + (place ^ j) * 2 + core - me
            m = jnp.where(m < 0, m + n, m)
            for c in range(cap):
                slot = m * cap + c
                target[core, c] = fold(acc, slot) + near[slot]

    for j in range(PLACES):
        lax.fori_loop(1, groups, lambda step, carry, j=j: pack(j, step, far_slots[j].at[step - 1]) or carry, 0)
        pack(j, 0, own_slots[j])


def combine_kernel(n, cap, first, count, me_ref, table, *refs):
    slots, (mine, other) = refs[:PLACES], refs[PLACES:]
    groups = n // GROUP
    me = me_ref[0]
    core = lax.rem(me, 2)
    group = me // GROUP

    def gather(step, carry):
        at = group + first + step
        at = jnp.where(at >= groups, at - groups, at)
        for target, side in ((mine, core), (other, 1 - core)):
            entry = (at ^ group) * 2 + (side ^ core)
            target[step] = jnp.zeros_like(target[step])
            for j in range(PLACES):
                m = at * GROUP + side - (group * GROUP + core) - ((place_of(me) ^ j) - place_of(me)) * 2
                m = jnp.where(m < 0, m + n, m)
                m = jnp.where(m >= n, m - n, m)
                for c in range(cap):
                    target[step, table[entry * cap + c, m]] += slots[j][step, side, c]
        return carry

    lax.fori_loop(0, count, gather, 0)


def place_of(me):
    return lax.rem(me // 2, PLACES)


def final_kernel(*refs):
    parts, out_ref, total = refs[:-2], refs[-2], refs[-1]
    value = parts[0][...]
    for part in parts[1:]:
        value = value + part[...]
    total[...] = value.reshape(TO * HALF, LANES)
    for r in range(HALF):
        out_ref[:, r * LANES : (r + 1) * LANES] = total[pl.ds(r, TO, stride=HALF), :]


def spec(space):
    return pl.BlockSpec(memory_space=space)


def body(a_blocks, p_blocks, a_slot, serve_rows, row_count, contrib_slot, recv_tile):
    n = lax.axis_size("elem")
    rows, blocks, _ = a_blocks.shape
    cap = recv_tile.shape[2]
    serve_count = serve_rows.shape[2]
    f32, i32, bf16 = jnp.float32, jnp.int32, jnp.bfloat16
    smem, vmem, hbm = spec(pltpu.SMEM), spec(pltpu.VMEM), spec(pl.ANY)
    pinned = n <= 32
    me = lax.axis_index("elem").astype(i32).reshape(1)

    def shape(dims, dtype):
        return pltpu.VMEM(dims, dtype) if pinned else jax.ShapeDtypeStruct(dims, dtype)

    def pin(value):
        return pltpu.with_memory_space_constraint(value, pltpu.VMEM) if pinned else value

    def pin_hbm(value):
        return pltpu.with_memory_space_constraint(value, pltpu.HBM)

    def across(value, partner):
        return lax.ppermute(value, "elem", [(i, partner(i)) for i in range(n)])

    p_view = p_blocks.reshape(rows, 2, HALF, LANES).transpose(0, 2, 1, 3).reshape(rows, B, LANES)
    own, send = pl.pallas_call(
        functools.partial(prep_kernel, n),
        out_shape=(shape((rows, B, LANES), f32), pltpu.HBM((n, serve_count, B, LANES), f32)),
        in_specs=[smem, hbm, hbm],
        out_specs=(vmem, hbm),
        scratch_shapes=[
            pltpu.VMEM((rows, B, LANES), f32),
            pltpu.SMEM((serve_count, n - 1), i32),
            pltpu.SemaphoreType.DMA((CHUNKS,)),
            pltpu.SemaphoreType.DMA,
            pltpu.SemaphoreType.DMA,
        ],
        compiler_params=params(8),
        name="prep",
    )(me, pin_hbm(serve_rows[0].T), pin_hbm(p_view))

    recv = lax.all_to_all(
        send.reshape(n, serve_count * B, LANES), "elem", split_axis=0, concat_axis=0, tiled=True
    ).reshape(n * serve_count, B, LANES)

    table = recv_tile.transpose(0, 2, 1)
    for flip in [1] + [GROUP << i for i in range((n // GROUP).bit_length() - 1)]:
        table = jnp.concatenate([table, across(table, lambda i, flip=flip: i ^ flip)], axis=0)
    table = table.reshape(n // PLACES * cap, n)

    entries = rows * blocks
    slot_count = n * cap
    meta_size = (entries + 2 * UNROLL) * META
    a_tiles = a_blocks.reshape(rows, blocks, HALF, LANES)
    left, near_slots, meta = pl.pallas_call(
        functools.partial(near_kernel, n),
        grid=(rows,),
        out_shape=(
            pltpu.HBM((entries, 2 * B, LANES), bf16),
            pltpu.HBM((slot_count, HALF, LANES), f32),
            jax.ShapeDtypeStruct((meta_size,), i32),
        ),
        in_specs=[smem, smem, smem, smem, vmem, pl.BlockSpec((1, blocks, HALF, LANES), lambda i: (i, 0, 0, 0))],
        out_specs=(hbm, hbm, smem),
        scratch_shapes=[
            pltpu.VMEM((slot_count + 1, B, LANES), f32),
            pltpu.VMEM((entries, 2 * B, LANES), bf16),
            pltpu.VMEM((slot_count, HALF, LANES), f32),
            pltpu.SMEM((meta_size,), i32),
            pltpu.SemaphoreType.DMA((2,)),
        ],
        compiler_params=params(20 + n // 4, dimension_semantics=("arbitrary",)),
        cost_estimate=pl.CostEstimate(flops=8 * entries * 2 * B * LANES * LANES, bytes_accessed=16 << 20, transcendentals=0),
        name="near",
    )(row_count, a_slot.T, contrib_slot, me, pin(own), a_tiles)

    groups = n // GROUP
    slot_shapes = [shape((groups - 1, 2, cap, HALF, LANES), f32)] * PLACES + [shape((2, cap, HALF, LANES), f32)] * PLACES
    slots = pl.pallas_call(
        functools.partial(far_kernel, n, cap),
        out_shape=slot_shapes,
        in_specs=[smem, smem, hbm, vmem, hbm],
        out_specs=[vmem] * (2 * PLACES),
        scratch_shapes=[
            pltpu.VMEM((slot_count + 1, B, LANES), f32),
            pltpu.VMEM((slot_count, HALF, LANES), f32),
            pltpu.VMEM((RING, 2 * B, LANES), bf16),
            pltpu.SemaphoreType.DMA((RING,)),
            pltpu.SemaphoreType.DMA,
        ],
        compiler_params=params(16 + n // 4),
        cost_estimate=pl.CostEstimate(flops=4 * entries * 2 * B * LANES * LANES, bytes_accessed=16 << 20, transcendentals=0),
        name="far",
    )(me, meta, pin_hbm(left), pin(recv), pin_hbm(near_slots))

    def combine(first, count, parts):
        return pl.pallas_call(
            functools.partial(combine_kernel, n, cap, first, count),
            out_shape=[shape((count, TO, HALF, LANES), f32)] * 2,
            in_specs=[smem, smem] + [vmem] * PLACES,
            out_specs=[vmem] * 2,
            compiler_params=params(8 + n // 4),
            name="combine",
        )(me, table, *[pin(part) for part in parts])

    far_slots = [slots[0]] + [across(slots[j], lambda i, j=j: i ^ (2 * j)) for j in range(1, PLACES)]
    mine, other = combine(1, groups - 1, far_slots)
    got = across(other, lambda i: i ^ 1)
    parts = [
        across(mine[step - 1] + got[step - 1], lambda i, step=step: (i + step * GROUP) % n) for step in range(1, groups)
    ]
    own_slots = [slots[PLACES]] + [across(slots[PLACES + j], lambda i, j=j: i ^ (2 * j)) for j in range(1, PLACES)]
    mine, other = combine(0, 1, [part[None] for part in own_slots])
    parts += [mine[0], across(other, lambda i: i ^ 1)[0]]

    return pl.pallas_call(
        final_kernel,
        out_shape=jax.ShapeDtypeStruct((TO, B * B), f32),
        in_specs=[vmem] * len(parts),
        out_specs=vmem,
        scratch_shapes=[pltpu.VMEM((TO * HALF, LANES), f32)],
        compiler_params=params(8),
        name="final",
    )(*[pin(part) for part in parts])


def solution(mesh):
    in_specs = (
        P("elem", None, None),
        P("elem", None, None),
        P("elem", None),
        P("elem", None, None),
        P("elem"),
        P("elem", None),
        P("elem", None, None),
    )
    out_specs = P("elem", None)
    return jax.shard_map(body, mesh=mesh, in_specs=in_specs, out_specs=out_specs, check_vma=False)
```

```python
import functools

import jax
import jax.numpy as jnp
from jax import lax
from jax.experimental import pallas as pl
from jax.experimental.pallas import tpu as pltpu
from jax.sharding import PartitionSpec as P

B = 64
HALF = B // 2
LANES = 2 * B
TO = 8
PLACES = 4
GROUP = 2 * PLACES
CHUNKS = 4
RING = 16
UNROLL = 4
META = 8
MIB = 1 << 20


def low_lanes(rows):
    return lax.broadcasted_iota(jnp.int32, (rows, LANES), 1) < B


def split_rows(value):
    high = value.astype(jnp.bfloat16)
    low = (value - high.astype(jnp.float32)).astype(jnp.bfloat16)
    return jnp.concatenate([high, high, low, low], axis=0)


def params(mib, **more):
    return pltpu.CompilerParams(vmem_limit_bytes=mib * MIB, **more)


def prep_kernel(n, me_ref, serve_hbm, p_hbm, own, send_hbm, p_ref, serve_ref, p_sems, serve_sem, send_sem):
    rows = p_ref.shape[0]
    serve_count = serve_ref.shape[0]
    mask = low_lanes(HALF)
    chunk = rows // CHUNKS

    def chunk_copy(i):
        part = pl.ds(i * chunk, chunk)
        return pltpu.make_async_copy(p_hbm.at[part], p_ref.at[part], p_sems.at[i])

    serve_copy = pltpu.make_async_copy(serve_hbm, serve_ref, serve_sem)
    for i in range(CHUNKS):
        chunk_copy(i).start()
    serve_copy.start()

    def relayout(i, carry):
        first = p_ref[i, pl.ds(0, HALF, stride=2), :]
        second = p_ref[i, pl.ds(1, HALF, stride=2), :]
        turned = pltpu.roll(jnp.where(mask, second, first), B, 1)
        own[i, pl.ds(0, HALF, stride=2), :] = jnp.where(mask, first, turned)
        own[i, pl.ds(1, HALF, stride=2), :] = jnp.where(mask, turned, second)
        return carry

    for i in range(CHUNKS):
        chunk_copy(i).wait()
        lax.fori_loop(i * chunk, (i + 1) * chunk, relayout, 0, unroll=4)
    serve_copy.wait()
    me = me_ref[0]

    def serve(target, carry):
        offset = target - me - 1
        offset = jnp.where(offset < 0, offset + n, offset)
        offset = jnp.minimum(offset, n - 2)
        for c in range(serve_count):
            pltpu.make_async_copy(own.at[serve_ref[c, offset]], send_hbm.at[target, c], send_sem).start()
        return carry

    lax.fori_loop(0, n, serve, 0, unroll=4)
    pltpu.make_async_copy(send_hbm, send_hbm, send_sem).wait()


def add_products(acc, out, dest):
    mask = low_lanes(B)
    for p in range(2):
        rows = out[p * B : (p + 1) * B]
        left = jnp.where(mask, rows, 0.0)
        acc[dest[2 * p]] += left
        acc[dest[2 * p + 1]] += rows - left


def fold(acc, slot):
    mask = low_lanes(HALF)
    even = acc[slot, pl.ds(0, HALF, stride=2), :]
    odd = acc[slot, pl.ds(1, HALF, stride=2), :]
    return jnp.where(mask, even, odd) + pltpu.roll(jnp.where(mask, odd, even), B, 1)


def near_kernel(
    n, count_row, a_slot, contrib, me_ref, own_ref, a_ref, left_hbm, slots_hbm, meta_ref, acc, left_ref, slots_ref, near_meta, sems
):
    step = pl.program_id(0)
    rows = own_ref.shape[0]
    blocks = a_ref.shape[1]
    slot_count = slots_ref.shape[0]
    per_row = contrib.shape[1] // 2

    @pl.when(step == 0)
    def start():
        acc[...] = jnp.zeros_like(acc)

    mask = low_lanes(HALF)
    y_even = own_ref[step, pl.ds(0, HALF, stride=2), :]
    y_odd = own_ref[step, pl.ds(1, HALF, stride=2), :]
    p_rows = jnp.concatenate([y_even, y_odd], axis=0)
    high = p_rows.astype(jnp.bfloat16).astype(jnp.float32)
    pair = jnp.concatenate([high, p_rows - high], axis=0).T.astype(jnp.bfloat16)
    lhs = jnp.concatenate([pair, pair], axis=1)
    for k in range(blocks):
        tile = a_ref[0, k]
        turned = pltpu.roll(tile, B, 1)
        both = jnp.concatenate([jnp.where(mask, tile, turned), jnp.where(mask, turned, tile)], axis=0)
        left = jnp.dot(lhs, split_rows(both), preferred_element_type=jnp.float32)
        left_high = left.astype(jnp.bfloat16).astype(jnp.float32)
        packed = jnp.where(low_lanes(2 * B), left_high, left - left_high)
        left_ref[step * blocks + k] = packed.astype(jnp.bfloat16)
    part = pl.ds(step * blocks, blocks)
    pltpu.make_async_copy(left_ref.at[part], left_hbm.at[part], sems.at[0]).start()

    @pl.when(step == pl.num_programs(0) - 1)
    def own_products():
        me = me_ref[0]
        live = count_row[0]

        def put(ref, at, f, row, i, k):
            ref[at * META] = f
            ref[at * META + 1] = row
            for p in range(2):
                for q in range(2):
                    ref[at * META + 2 + 2 * p + q] = contrib[i, p * per_row + 2 * k + q]

        def put_pad(ref, at):
            ref[at * META] = 0
            ref[at * META + 1] = 0
            for j in range(4):
                ref[at * META + 2 + j] = slot_count

        def scan_row(i, carry):
            near_count, far_count = carry
            for k in range(blocks):
                slot = a_slot[k, i]
                is_near = slot < rows
                index = slot - rows
                source = me - 1 - index // 2
                source = jnp.where(source < 0, source + n, source)
                f = i * blocks + k
                put(near_meta, near_count, f, jnp.where(is_near, slot, 0), i, k)
                put(meta_ref, far_count, f, jnp.where(is_near, 0, source * 2 + index % 2), i, k)
                near_count = near_count + jnp.where(is_near, 1, 0)
                far_count = far_count + jnp.where(is_near, 0, 1)
            return near_count, far_count

        near_count, far_count = lax.fori_loop(0, jnp.minimum(live, rows), scan_row, (0, 0))
        for j in range(UNROLL):
            put_pad(near_meta, near_count + j)
            put_pad(meta_ref, far_count + j)
        meta_ref[meta_ref.shape[0] - 1] = far_count

        def products(g, carry):
            for u in range(UNROLL):
                at = (g * UNROLL + u) * META
                lp = left_ref[near_meta[at]]
                weights = split_rows(own_ref[near_meta[at + 1]])
                out = jnp.dot(jnp.concatenate([lp, lp], axis=1), weights, preferred_element_type=jnp.float32)
                add_products(acc, out, [near_meta[at + 2 + j] for j in range(4)])
            return carry

        lax.fori_loop(0, (near_count + UNROLL - 1) // UNROLL, products, 0)

        def pack(slot, carry):
            slots_ref[slot] = fold(acc, slot)
            return carry

        lax.fori_loop(0, slot_count, pack, 0, unroll=2)
        slots_copy = pltpu.make_async_copy(slots_ref, slots_hbm, sems.at[1])
        slots_copy.start()
        pltpu.make_async_copy(left_hbm, left_hbm, sems.at[0]).wait()
        slots_copy.wait()


def far_kernel(n, cap, me_ref, meta, left_hbm, recv, near_hbm, *refs):
    far_slots, own_mine, own_other = refs[:PLACES], refs[PLACES], refs[PLACES + 1]
    acc, near, ring, ring_sems, near_sem = refs[PLACES + 2 :]
    me = me_ref[0]
    count = meta[meta.shape[0] - 1]
    turns = (count + UNROLL - 1) // UNROLL
    depth = RING // UNROLL

    def fetch(g):
        @pl.when(g < turns)
        def go():
            for u in range(UNROLL):
                buffer = lax.rem(g, depth) * UNROLL + u
                source = left_hbm.at[meta[(g * UNROLL + u) * META]]
                pltpu.make_async_copy(source, ring.at[buffer], ring_sems.at[buffer]).start()

    for g in range(depth - 1):
        fetch(g)
    near_copy = pltpu.make_async_copy(near_hbm, near, near_sem)
    near_copy.start()
    acc[...] = jnp.zeros_like(acc)

    def products(g, carry):
        fetch(g + depth - 1)
        for u in range(UNROLL):
            buffer = lax.rem(g, depth) * UNROLL + u
            pltpu.make_async_copy(left_hbm.at[0], ring.at[buffer], ring_sems.at[buffer]).wait()
        for u in range(UNROLL):
            at = (g * UNROLL + u) * META
            lp = ring[lax.rem(g, depth) * UNROLL + u]
            weights = split_rows(recv[meta[at + 1]])
            out = jnp.dot(jnp.concatenate([lp, lp], axis=1), weights, preferred_element_type=jnp.float32)
            add_products(acc, out, [meta[at + 2 + j] for j in range(4)])
        return carry

    lax.fori_loop(0, turns, products, 0)
    near_copy.wait()
    groups = n // GROUP
    place = lax.rem(me // 2, PLACES)
    group = me // GROUP

    core = lax.rem(me, 2)

    def pack(j, step, side, target):
        at = group + step
        at = jnp.where(at >= groups, at - groups, at)
        m = at * GROUP + (place ^ j) * 2 + side - me
        m = jnp.where(m < 0, m + n, m)
        for c in range(cap):
            slot = m * cap + c
            target[c] = fold(acc, slot) + near[slot]

    def pack_far(step, carry):
        for j in range(PLACES):
            for side in range(2):
                pack(j, step, side, far_slots[j].at[step - 1, side])
        return carry

    lax.fori_loop(1, groups, pack_far, 0)
    for j in range(PLACES):
        pack(j, 0, core, own_mine.at[j])
        pack(j, 0, 1 - core, own_other.at[j])


def add_slots(target, table, entry, m, slots):
    for c in range(slots.shape[0]):
        target[table[entry * slots.shape[0] + c, m]] += slots[c]


def combine_far_kernel(n, me_ref, table, *refs):
    slots, (mine, other) = refs[:PLACES], refs[PLACES:]
    groups = n // GROUP
    me = me_ref[0]
    core = lax.rem(me, 2)
    place = lax.rem(me // 2, PLACES)
    group = me // GROUP

    def gather(step, carry):
        at = group + step
        at = jnp.where(at >= groups, at - groups, at)
        for target, side in ((mine, core), (other, 1 - core)):
            tiles = target.at[step - 1]
            tiles[...] = jnp.zeros_like(tiles)
            for j in range(PLACES):
                m = (at - group) * GROUP + (place - (place ^ j)) * 2 + side - core
                m = jnp.where(m < 0, m + n, m)
                add_slots(tiles, table, (at ^ group) * 2 + (side ^ core), m, slots[j].at[step - 1, side])
        return carry

    lax.fori_loop(1, groups, gather, 0)


def combine_own_kernel(n, me_ref, table, mine, got, *tiles):
    me = me_ref[0]
    core = lax.rem(me, 2)
    place = lax.rem(me // 2, PLACES)
    for j in range(PLACES):
        tiles[j][...] = jnp.zeros_like(tiles[j])
        for other, slots in ((0, mine), (1, got)):
            m = ((place ^ j) - place) * 2 + other * (2 * core - 1)
            m = jnp.where(m < 0, m + n, m)
            add_slots(tiles[j], table, j, m, slots.at[j])


def final_kernel(*refs):
    parts, out_ref, total = refs[:-2], refs[-2], refs[-1]
    value = parts[0][...]
    for part in parts[1:]:
        value = value + part[...]
    total[...] = value.reshape(TO * HALF, LANES)
    for r in range(HALF):
        out_ref[:, r * LANES : (r + 1) * LANES] = total[pl.ds(r, TO, stride=HALF), :]


def spec(space):
    return pl.BlockSpec(memory_space=space)


def body(a_blocks, p_blocks, a_slot, serve_rows, row_count, contrib_slot, recv_tile):
    n = lax.axis_size("elem")
    rows, blocks, _ = a_blocks.shape
    cap = recv_tile.shape[2]
    serve_count = serve_rows.shape[2]
    f32, i32, bf16 = jnp.float32, jnp.int32, jnp.bfloat16
    smem, vmem, hbm = spec(pltpu.SMEM), spec(pltpu.VMEM), spec(pl.ANY)
    pinned = n <= 32
    me = lax.axis_index("elem").astype(i32).reshape(1)

    def shape(dims, dtype):
        return pltpu.VMEM(dims, dtype) if pinned else jax.ShapeDtypeStruct(dims, dtype)

    def pin(value):
        return pltpu.with_memory_space_constraint(value, pltpu.VMEM) if pinned else value

    def pin_hbm(value):
        return pltpu.with_memory_space_constraint(value, pltpu.HBM)

    def across(value, partner):
        return lax.ppermute(value, "elem", [(i, partner(i)) for i in range(n)])

    p_view = p_blocks.reshape(rows, 2, HALF, LANES).transpose(0, 2, 1, 3).reshape(rows, B, LANES)
    own, send = pl.pallas_call(
        functools.partial(prep_kernel, n),
        out_shape=(shape((rows, B, LANES), f32), pltpu.HBM((n, serve_count, B, LANES), f32)),
        in_specs=[smem, hbm, hbm],
        out_specs=(vmem, hbm),
        scratch_shapes=[
            pltpu.VMEM((rows, B, LANES), f32),
            pltpu.SMEM((serve_count, n - 1), i32),
            pltpu.SemaphoreType.DMA((CHUNKS,)),
            pltpu.SemaphoreType.DMA,
            pltpu.SemaphoreType.DMA,
        ],
        compiler_params=params(8),
        name="prep",
    )(me, pin_hbm(serve_rows[0].T), pin_hbm(p_view))

    recv = lax.all_to_all(
        send.reshape(n, serve_count * B, LANES), "elem", split_axis=0, concat_axis=0, tiled=True
    ).reshape(n * serve_count, B, LANES)

    table = recv_tile.transpose(0, 2, 1)
    own_table = jnp.concatenate([table] + [across(table, lambda i, j=j: i ^ (2 * j)) for j in range(1, PLACES)], axis=0)
    far_table = jnp.concatenate([table, across(table, lambda i: i ^ 1)], axis=0)
    recv, own_table, far_table = lax.optimization_barrier((recv, own_table, far_table))
    for flip in [GROUP << i for i in range((n // GROUP).bit_length() - 1)]:
        far_table = jnp.concatenate([far_table, across(far_table, lambda i, flip=flip: i ^ flip)], axis=0)
    own_table, far_table = own_table.reshape(-1, n), far_table.reshape(-1, n)

    entries = rows * blocks
    slot_count = n * cap
    meta_size = (entries + 2 * UNROLL) * META
    a_tiles = a_blocks.reshape(rows, blocks, HALF, LANES)
    left, near_slots, meta = pl.pallas_call(
        functools.partial(near_kernel, n),
        grid=(rows,),
        out_shape=(
            pltpu.HBM((entries, 2 * B, LANES), bf16),
            pltpu.HBM((slot_count, HALF, LANES), f32),
            jax.ShapeDtypeStruct((meta_size,), i32),
        ),
        in_specs=[smem, smem, smem, smem, vmem, pl.BlockSpec((1, blocks, HALF, LANES), lambda i: (i, 0, 0, 0))],
        out_specs=(hbm, hbm, smem),
        scratch_shapes=[
            pltpu.VMEM((slot_count + 1, B, LANES), f32),
            pltpu.VMEM((entries, 2 * B, LANES), bf16),
            pltpu.VMEM((slot_count, HALF, LANES), f32),
            pltpu.SMEM((meta_size,), i32),
            pltpu.SemaphoreType.DMA((2,)),
        ],
        compiler_params=params(20 + n // 4, dimension_semantics=("arbitrary",)),
        cost_estimate=pl.CostEstimate(flops=8 * entries * 2 * B * LANES * LANES, bytes_accessed=16 << 20, transcendentals=0),
        name="near",
    )(row_count, a_slot.T, contrib_slot, me, pin(own), a_tiles)

    groups = n // GROUP
    slot_shapes = [shape((groups - 1, 2, cap, HALF, LANES), f32)] * PLACES + [shape((PLACES, cap, HALF, LANES), f32)] * 2
    slots = pl.pallas_call(
        functools.partial(far_kernel, n, cap),
        out_shape=slot_shapes,
        in_specs=[smem, smem, hbm, vmem, hbm],
        out_specs=[vmem] * (PLACES + 2),
        scratch_shapes=[
            pltpu.VMEM((slot_count + 1, B, LANES), f32),
            pltpu.VMEM((slot_count, HALF, LANES), f32),
            pltpu.VMEM((RING, 2 * B, LANES), bf16),
            pltpu.SemaphoreType.DMA((RING,)),
            pltpu.SemaphoreType.DMA,
        ],
        compiler_params=params(16 + n // 4),
        cost_estimate=pl.CostEstimate(flops=4 * entries * 2 * B * LANES * LANES, bytes_accessed=16 << 20, transcendentals=0),
        name="far",
    )(me, meta, pin_hbm(left), pin(recv), pin_hbm(near_slots))

    def combine(kernel, out_shape, table, parts):
        return pl.pallas_call(
            functools.partial(kernel, n),
            out_shape=out_shape,
            in_specs=[smem, smem] + [vmem] * len(parts),
            out_specs=[vmem] * len(out_shape),
            compiler_params=params(8 + n // 4),
            name=kernel.__name__,
        )(me, table, *[pin(part) for part in parts])

    far_slots = [slots[0]] + [across(slots[j], lambda i, j=j: i ^ (2 * j)) for j in range(1, PLACES)]
    own_mine, own_other = slots[PLACES:]
    own_shape = [shape((TO, HALF, LANES), f32)] * PLACES
    own_tiles = combine(combine_own_kernel, own_shape, own_table, [own_mine, across(own_other, lambda i: i ^ 1)])
    far_shape = [shape((groups - 1, TO, HALF, LANES), f32)] * 2
    mine, other = combine(combine_far_kernel, far_shape, far_table, far_slots)
    got = across(other, lambda i: i ^ 1)
    summed = [mine[step] + got[step] for step in range(groups - 1)]
    summed, own_tiles = lax.optimization_barrier((summed, own_tiles))
    parts = [across(value, lambda i, step=step: (i + step * GROUP) % n) for step, value in enumerate(summed, 1)]
    parts += [own_tiles[0]] + [across(own_tiles[j], lambda i, j=j: i ^ (2 * j)) for j in range(1, PLACES)]

    return pl.pallas_call(
        final_kernel,
        out_shape=jax.ShapeDtypeStruct((TO, B * B), f32),
        in_specs=[vmem] * len(parts),
        out_specs=vmem,
        scratch_shapes=[pltpu.VMEM((TO * HALF, LANES), f32)],
        compiler_params=params(8),
        name="final",
    )(*[pin(part) for part in parts])


def solution(mesh):
    in_specs = (
        P("elem", None, None),
        P("elem", None, None),
        P("elem", None),
        P("elem", None, None),
        P("elem"),
        P("elem", None),
        P("elem", None, None),
    )
    out_specs = P("elem", None)
    return jax.shard_map(body, mesh=mesh, in_specs=in_specs, out_specs=out_specs, check_vma=False)
```

```python
import functools

import jax
import jax.numpy as jnp
from jax import lax
from jax.experimental import pallas as pl
from jax.experimental.pallas import tpu as pltpu
from jax.sharding import PartitionSpec as P

B = 64
HALF = B // 2
LANES = 2 * B
TO = 8
PLACES = 4
GROUP = 2 * PLACES
CHUNKS = 4
FIRST = 24
REST = HALF - FIRST
DEPTH = 3
UNROLL = 16
META = 8
MIB = 1 << 20


def low_lanes(rows):
    return lax.broadcasted_iota(jnp.int32, (rows, LANES), 1) < B


def split_rows(value):
    high = value.astype(jnp.bfloat16)
    low = (value - high.astype(jnp.float32)).astype(jnp.bfloat16)
    return jnp.concatenate([high, high, low, low], axis=0)


def params(mib, **more):
    return pltpu.CompilerParams(vmem_limit_bytes=mib * MIB, **more)


def prep_kernel(n, me_ref, serve_hbm, p_hbm, own, send_hbm, p_ref, send, serve_ref, p_sems, serve_sem, send_sems):
    rows = p_ref.shape[0]
    serve_count = serve_ref.shape[0]
    mask = low_lanes(HALF)
    chunk = rows // CHUNKS

    def chunk_copy(i):
        part = pl.ds(i * chunk, chunk)
        return pltpu.make_async_copy(p_hbm.at[part], p_ref.at[part], p_sems.at[i])

    serve_copy = pltpu.make_async_copy(serve_hbm, serve_ref, serve_sem)
    for i in range(CHUNKS):
        chunk_copy(i).start()
    serve_copy.start()

    def relayout(i, carry):
        first = p_ref[i, pl.ds(0, HALF, stride=2), :]
        second = p_ref[i, pl.ds(1, HALF, stride=2), :]
        turned = pltpu.roll(jnp.where(mask, second, first), B, 1)
        own[i, pl.ds(0, HALF, stride=2), :] = jnp.where(mask, first, turned)
        own[i, pl.ds(1, HALF, stride=2), :] = jnp.where(mask, turned, second)
        return carry

    for i in range(CHUNKS):
        chunk_copy(i).wait()
        lax.fori_loop(i * chunk, (i + 1) * chunk, relayout, 0, unroll=4)
    serve_copy.wait()
    me = me_ref[0]

    targets = n // CHUNKS

    def serve(target, carry):
        offset = target - me - 1
        offset = jnp.where(offset < 0, offset + n, offset)
        offset = jnp.minimum(offset, n - 2)
        for c in range(serve_count):
            send[target, c] = own[serve_ref[c, offset]]
        return carry

    def send_copy(i):
        part = pl.ds(i * targets, targets)
        return pltpu.make_async_copy(send.at[part], send_hbm.at[part], send_sems.at[i])

    for i in range(CHUNKS):
        lax.fori_loop(i * targets, (i + 1) * targets, serve, 0, unroll=4)
        send_copy(i).start()
    for i in range(CHUNKS):
        send_copy(i).wait()


def add_products(acc, out, dest):
    mask = low_lanes(B)
    for p in range(2):
        rows = out[p * B : (p + 1) * B]
        left = jnp.where(mask, rows, 0.0)
        acc[dest[2 * p]] += left
        acc[dest[2 * p + 1]] += rows - left


def add_entry(acc, meta, e, lp, right_ref):
    weights = split_rows(right_ref[meta[e * META]])
    out = jnp.dot(jnp.concatenate([lp, lp], axis=1), weights, preferred_element_type=jnp.float32)
    add_products(acc, out, [meta[e * META + 1 + j] for j in range(4)])


def fold(acc, slot):
    mask = low_lanes(HALF)
    even, odd = acc[slot, :HALF], acc[slot, HALF:]
    return jnp.where(mask, even, odd) + pltpu.roll(jnp.where(mask, odd, even), B, 1)


def near_kernel(
    n, count_row, a_slot, contrib, me_ref, own_ref, a_ref, left_hbm, slots_hbm, meta_ref, acc, left_ref, slots_ref, turned_rows, near_meta, place_of, sems
):
    step = pl.program_id(0)
    rows = own_ref.shape[0]
    blocks = a_ref.shape[1]
    slot_count = slots_ref.shape[0]
    per_row = contrib.shape[1] // 2
    entries = rows * blocks
    last = near_meta.shape[0] - 1

    @pl.when(step == 0)
    def start():
        me = me_ref[0]

        def put(ref, at, row, i, k):
            ref[at * META] = row
            for p in range(2):
                for q in range(2):
                    ref[at * META + 1 + 2 * p + q] = contrib[i, p * per_row + 2 * k + q]

        def put_pad(ref, at):
            ref[at * META] = 0
            for j in range(4):
                ref[at * META + 1 + j] = slot_count

        def scan_row(i, carry):
            near_count, far_count = carry
            for k in range(blocks):
                slot = a_slot[k, i]
                is_near = slot < rows
                index = slot - rows
                source = me - 1 - index // 2
                source = jnp.where(source < 0, source + n, source)
                put(near_meta, near_count, jnp.where(is_near, slot, 0), i, k)
                put(meta_ref, far_count, jnp.where(is_near, 0, source * 2 + index % 2), i, k)
                place_of[i * blocks + k] = jnp.where(is_near, entries - 1 - near_count, far_count)
                near_count = near_count + jnp.where(is_near, 1, 0)
                far_count = far_count + jnp.where(is_near, 0, 1)
            return near_count, far_count

        def skip_row(i, carry):
            for k in range(blocks):
                place_of[i * blocks + k] = entries
            return carry

        live = jnp.minimum(count_row[0], rows)
        near_count, far_count = lax.fori_loop(0, live, scan_row, (0, 0))
        lax.fori_loop(live, rows, skip_row, 0)
        for j in range(UNROLL):
            put_pad(near_meta, near_count + j)
            put_pad(meta_ref, far_count + j)
        near_meta[last] = near_count
        meta_ref[last] = far_count
        acc[...] = jnp.zeros_like(acc)

    mask = low_lanes(HALF)
    y_even = own_ref[step, pl.ds(0, HALF, stride=2), :]
    y_odd = own_ref[step, pl.ds(1, HALF, stride=2), :]
    p_rows = jnp.concatenate([y_even, y_odd], axis=0)
    high = p_rows.astype(jnp.bfloat16).astype(jnp.float32)
    turned_rows[...] = jnp.concatenate([high, p_rows - high], axis=0).T
    pair = [turned_rows[pl.ds(p * B + parity, HALF, stride=2), :] for p in range(2) for parity in range(2)]
    pair = jnp.concatenate(pair, axis=0).astype(jnp.bfloat16)
    lhs = jnp.concatenate([pair, pair], axis=1)
    for k in range(blocks):
        tile = a_ref[0, k]
        turned = pltpu.roll(tile, B, 1)
        both = jnp.concatenate([jnp.where(mask, tile, turned), jnp.where(mask, turned, tile)], axis=0)
        left = jnp.dot(lhs, split_rows(both), preferred_element_type=jnp.float32)
        left_high = left.astype(jnp.bfloat16).astype(jnp.float32)
        packed = jnp.where(low_lanes(2 * B), left_high, left - left_high)
        left_ref[place_of[step * blocks + k]] = packed.astype(jnp.bfloat16)

    @pl.when(step == pl.num_programs(0) - 1)
    def own_products():
        left_copy = pltpu.make_async_copy(left_ref, left_hbm, sems.at[0])
        left_copy.start()

        def products(g, carry):
            for u in range(UNROLL):
                e = g * UNROLL + u
                add_entry(acc, near_meta, e, left_ref[jnp.maximum(entries - 1 - e, 0)], own_ref)
            return carry

        lax.fori_loop(0, (near_meta[last] + UNROLL - 1) // UNROLL, products, 0)

        def pack(slot, carry):
            slots_ref[slot] = fold(acc, slot)
            return carry

        lax.fori_loop(0, slot_count, pack, 0, unroll=8)
        slots_copy = pltpu.make_async_copy(slots_ref, slots_hbm, sems.at[1])
        slots_copy.start()
        left_copy.wait()
        slots_copy.wait()


def far_kernel(n, cap, me_ref, meta, left_hbm, recv, near_hbm, *refs):
    groups = n // GROUP
    far_slots, rest_slots = refs[:PLACES], refs[PLACES : PLACES + groups - 1]
    own_mine, own_other, acc, near, ring, ring_sems, near_sem = refs[PLACES + groups - 1 :]
    me = me_ref[0]
    count = meta[meta.shape[0] - 1]
    turns = (count + UNROLL - 1) // UNROLL

    def left_copy(g):
        buffer = lax.rem(g, DEPTH)
        return pltpu.make_async_copy(left_hbm.at[pl.ds(g * UNROLL, UNROLL)], ring.at[buffer], ring_sems.at[buffer])

    def fetch(g):
        @pl.when(g < turns)
        def go():
            left_copy(g).start()

    for g in range(DEPTH - 1):
        fetch(g)
    near_copy = pltpu.make_async_copy(near_hbm, near, near_sem)
    near_copy.start()
    acc[...] = jnp.zeros_like(acc)

    def products(g, carry):
        fetch(g + DEPTH - 1)
        left_copy(g).wait()
        for u in range(UNROLL):
            add_entry(acc, meta, g * UNROLL + u, ring[lax.rem(g, DEPTH), u], recv)
        return carry

    lax.fori_loop(0, turns, products, 0)
    near_copy.wait()
    place = lax.rem(me // 2, PLACES)
    group = me // GROUP

    core = lax.rem(me, 2)

    def packed(j, step, side):
        at = group + step
        at = jnp.where(at >= groups, at - groups, at)
        m = at * GROUP + (place ^ j) * 2 + side - me
        m = jnp.where(m < 0, m + n, m)
        return [fold(acc, m * cap + c) + near[m * cap + c] for c in range(cap)]

    for j in range(PLACES):
        for other in range(2):
            side = 1 - core if other else core
            for step in range(1, groups):
                for c, slot in enumerate(packed(j, step, side)):
                    far_slots[j][step - 1, side, c] = slot[:FIRST]
                    rest_slots[step - 1][other, j, c] = slot[FIRST:]
            for c, slot in enumerate(packed(j, 0, side)):
                (own_other if other else own_mine)[j, c] = slot


def add_slots(target, table, entry, m, slots, first=0):
    for c in range(slots.shape[0]):
        target[table[entry * slots.shape[0] + c, m], pl.ds(first, slots.shape[1]), :] += slots[c]


def combine_far_kernel(n, me_ref, table, *refs):
    slots, (mine, other) = refs[:PLACES], refs[PLACES:]
    groups = n // GROUP
    me = me_ref[0]
    core = lax.rem(me, 2)
    place = lax.rem(me // 2, PLACES)
    group = me // GROUP

    def gather(step, carry):
        at = group + step
        at = jnp.where(at >= groups, at - groups, at)
        for target, side in ((mine, core), (other, 1 - core)):
            tiles = target.at[step - 1]
            tiles[...] = jnp.zeros_like(tiles)
            for j in range(PLACES):
                m = (at - group) * GROUP + (place - (place ^ j)) * 2 + side - core
                m = jnp.where(m < 0, m + n, m)
                add_slots(tiles, table, (at ^ group) * 2 + (side ^ core), m, slots[j].at[step - 1, side])
        return carry

    lax.fori_loop(1, groups, gather, 0)


def combine_own_kernel(n, me_ref, table, mine, got, rest_got, *refs):
    rest_mine, tiles = refs[:-PLACES], refs[-PLACES:]
    me = me_ref[0]
    core = lax.rem(me, 2)
    place = lax.rem(me // 2, PLACES)
    for j in range(PLACES):
        tiles[j][...] = jnp.zeros_like(tiles[j])
        for other in range(2):
            m = ((place ^ j) - place) * 2 + other * (2 * core - 1)
            m = jnp.where(m < 0, m + n, m)
            add_slots(tiles[j], table, j, m, (got if other else mine).at[j])
            for step, rest in enumerate(rest_mine, 1):
                at = m + step * GROUP
                at = jnp.where(at >= n, at - n, at)
                add_slots(tiles[j], table, j, at, rest_got.at[step - 1, j] if other else rest.at[0, j], FIRST)


def final_kernel(*refs):
    own, far, out_ref, total = refs[:PLACES], refs[PLACES:-2], refs[-2], refs[-1]
    for t in range(TO):
        total[t * HALF : (t + 1) * HALF] = own[0][t] + own[1][t] + own[2][t] + own[3][t]
        value = far[0][t]
        for part in far[1:]:
            value = value + part[t]
        total[t * HALF : t * HALF + FIRST] += value
    for r in range(HALF):
        out_ref[:, r * LANES : (r + 1) * LANES] = total[pl.ds(r, TO, stride=HALF), :]


def spec(space):
    return pl.BlockSpec(memory_space=space)


def body(a_blocks, p_blocks, a_slot, serve_rows, row_count, contrib_slot, recv_tile):
    n = lax.axis_size("elem")
    rows, blocks, _ = a_blocks.shape
    cap = recv_tile.shape[2]
    serve_count = serve_rows.shape[2]
    f32, i32, bf16 = jnp.float32, jnp.int32, jnp.bfloat16
    smem, vmem, hbm = spec(pltpu.SMEM), spec(pltpu.VMEM), spec(pl.ANY)
    pinned = n <= 32
    me = lax.axis_index("elem").astype(i32).reshape(1)

    def shape(dims, dtype):
        return pltpu.VMEM(dims, dtype) if pinned else jax.ShapeDtypeStruct(dims, dtype)

    def pin(value):
        return pltpu.with_memory_space_constraint(value, pltpu.VMEM) if pinned else value

    def pin_hbm(value):
        return pltpu.with_memory_space_constraint(value, pltpu.HBM)

    def across(value, partner):
        return lax.ppermute(value, "elem", [(i, partner(i)) for i in range(n)])

    p_view = p_blocks.reshape(rows, 2, HALF, LANES).transpose(0, 2, 1, 3).reshape(rows, B, LANES)
    own, send = pl.pallas_call(
        functools.partial(prep_kernel, n),
        out_shape=(shape((rows, B, LANES), f32), pltpu.HBM((n, serve_count, B, LANES), f32)),
        in_specs=[smem, hbm, hbm],
        out_specs=(vmem, hbm),
        scratch_shapes=[
            pltpu.VMEM((rows, B, LANES), f32),
            pltpu.VMEM((n, serve_count, B, LANES), f32),
            pltpu.SMEM((serve_count, n - 1), i32),
            pltpu.SemaphoreType.DMA((CHUNKS,)),
            pltpu.SemaphoreType.DMA,
            pltpu.SemaphoreType.DMA((CHUNKS,)),
        ],
        compiler_params=params(8 + n // 8),
        name="prep",
    )(me, pin_hbm(serve_rows[0].T), pin_hbm(p_view))

    recv = lax.all_to_all(
        send.reshape(n, serve_count * B, LANES), "elem", split_axis=0, concat_axis=0, tiled=True
    ).reshape(n * serve_count, B, LANES)

    groups = n // GROUP
    table = recv_tile.transpose(0, 2, 1)
    own_table = jnp.concatenate([table] + [across(table, lambda i, j=j: i ^ (2 * j)) for j in range(1, PLACES)], axis=0)
    pair = jnp.concatenate([table, across(table, lambda i: i ^ 1)], axis=0)
    a_blocks, pair = lax.optimization_barrier((a_blocks, pair))
    far_table = jnp.concatenate(
        [pair] + [across(pair, lambda i, step=step: i ^ (step * GROUP)) for step in range(1, groups)], axis=0
    )
    recv, own_table, far_table = lax.optimization_barrier((recv, own_table, far_table))
    own_table, far_table = own_table.reshape(-1, n), far_table.reshape(-1, n)

    entries = rows * blocks
    slot_count = n * cap
    meta_size = (entries + 2 * UNROLL) * META
    a_tiles = a_blocks.reshape(rows, blocks, HALF, LANES)
    left, near_slots, meta = pl.pallas_call(
        functools.partial(near_kernel, n),
        grid=(rows,),
        out_shape=(
            pltpu.HBM((entries + UNROLL, 2 * B, LANES), bf16),
            pltpu.HBM((slot_count, HALF, LANES), f32),
            jax.ShapeDtypeStruct((meta_size,), i32),
        ),
        in_specs=[smem, smem, smem, smem, vmem, pl.BlockSpec((1, blocks, HALF, LANES), lambda i: (i, 0, 0, 0))],
        out_specs=(hbm, hbm, smem),
        scratch_shapes=[
            pltpu.VMEM((slot_count + 1, B, LANES), f32),
            pltpu.VMEM((entries + UNROLL, 2 * B, LANES), bf16),
            pltpu.VMEM((slot_count, HALF, LANES), f32),
            pltpu.VMEM((2 * B, LANES), f32),
            pltpu.SMEM((meta_size,), i32),
            pltpu.SMEM((entries,), i32),
            pltpu.SemaphoreType.DMA((2,)),
        ],
        compiler_params=params(20 + n // 4, dimension_semantics=("arbitrary",)),
        cost_estimate=pl.CostEstimate(flops=8 * entries * 2 * B * LANES * LANES, bytes_accessed=16 << 20, transcendentals=0),
        name="near",
    )(row_count, a_slot.T, contrib_slot, me, pin(own), a_tiles)

    slot_shapes = [shape((groups - 1, 2, cap, FIRST, LANES), f32)] * PLACES
    slot_shapes += [shape((2, PLACES, cap, REST, LANES), f32)] * (groups - 1)
    slot_shapes += [shape((PLACES, cap, HALF, LANES), f32)] * 2
    slots = pl.pallas_call(
        functools.partial(far_kernel, n, cap),
        out_shape=slot_shapes,
        in_specs=[smem, smem, hbm, vmem, hbm],
        out_specs=[vmem] * len(slot_shapes),
        scratch_shapes=[
            pltpu.VMEM((slot_count + 1, B, LANES), f32),
            pltpu.VMEM((slot_count, HALF, LANES), f32),
            pltpu.VMEM((DEPTH, UNROLL, 2 * B, LANES), bf16),
            pltpu.SemaphoreType.DMA((DEPTH,)),
            pltpu.SemaphoreType.DMA,
        ],
        compiler_params=params(16 + n // 4),
        cost_estimate=pl.CostEstimate(flops=4 * entries * 2 * B * LANES * LANES, bytes_accessed=16 << 20, transcendentals=0),
        name="far",
    )(me, meta, pin_hbm(left), pin(recv), pin_hbm(near_slots))

    def combine(kernel, out_shape, table, parts):
        return pl.pallas_call(
            functools.partial(kernel, n),
            out_shape=out_shape,
            in_specs=[smem, smem] + [vmem] * len(parts),
            out_specs=[vmem] * len(out_shape),
            compiler_params=params(8 + n // 4),
            name=kernel.__name__,
        )(me, table, *[pin(part) for part in parts])

    def in_group(values):
        return [values[0]] + [across(values[j], lambda i, j=j: i ^ (2 * j)) for j in range(1, PLACES)]

    def over_groups(values):
        return [across(value, lambda i, step=step: (i + step * GROUP) % n) for step, value in enumerate(values, 1)]

    def other_core(value):
        return across(value, lambda i: i ^ 1)

    own_mine, own_other = slots[-2:]
    rest = over_groups(slots[PLACES:-2])
    far_slots = in_group(slots[:PLACES])
    rest_got = other_core(jnp.stack([part[1] for part in rest]))
    own_shape = [shape((TO, HALF, LANES), f32)] * PLACES
    own_tiles = combine(combine_own_kernel, own_shape, own_table, [own_mine, other_core(own_other), rest_got] + rest)
    far_shape = [shape((groups - 1, TO, FIRST, LANES), f32)] * 2
    mine, other = combine(combine_far_kernel, far_shape, far_table, far_slots)
    got = other_core(other)
    summed = [mine[step] + got[step] for step in range(groups - 1)]
    summed, own_tiles = lax.optimization_barrier((summed, own_tiles))
    far_parts = over_groups(summed)
    parts = in_group(own_tiles) + far_parts

    return pl.pallas_call(
        final_kernel,
        out_shape=jax.ShapeDtypeStruct((TO, B * B), f32),
        in_specs=[vmem] * len(parts),
        out_specs=vmem,
        scratch_shapes=[pltpu.VMEM((TO * HALF, LANES), f32)],
        compiler_params=params(8),
        name="final",
    )(*[pin(part) for part in parts])


def solution(mesh):
    in_specs = (
        P("elem", None, None),
        P("elem", None, None),
        P("elem", None),
        P("elem", None, None),
        P("elem"),
        P("elem", None),
        P("elem", None, None),
    )
    out_specs = P("elem", None)
    return jax.shard_map(body, mesh=mesh, in_specs=in_specs, out_specs=out_specs, check_vma=False)
```

```python
import functools

import jax
import jax.numpy as jnp
from jax import lax
from jax.experimental import pallas as pl
from jax.experimental.pallas import tpu as pltpu
from jax.sharding import PartitionSpec as P

B = 64
HALF = B // 2
LANES = 2 * B
TO = 8
PLACES = 4
GROUP = 2 * PLACES
CHUNKS = 4
REST = HALF // 2
FETCH = 16
DEPTH = 6
UNROLL = 32
META = 8
MIB = 1 << 20


def low_lanes(rows):
    return lax.broadcasted_iota(jnp.int32, (rows, LANES), 1) < B


def split_rows(value):
    high = value.astype(jnp.bfloat16)
    low = (value - high.astype(jnp.float32)).astype(jnp.bfloat16)
    return jnp.concatenate([high, high, low, low], axis=0)


def split_steps(groups):
    steps, first = {}, 0
    for step in range(1, groups):
        rows = HALF if step == groups // 2 else HALF - REST
        steps[step] = first, rows
        first += rows
    return steps, first, [step for step, (_, rows) in steps.items() if rows < HALF]


def params(mib, **more):
    return pltpu.CompilerParams(vmem_limit_bytes=mib * MIB, **more)


def prep_kernel(n, me_ref, serve_hbm, p_hbm, own, send_hbm, p_ref, send, serve_ref, p_sems, serve_sem, send_sems):
    rows = p_ref.shape[0]
    serve_count = serve_ref.shape[0]
    mask = low_lanes(HALF)
    chunk = rows // CHUNKS

    def chunk_copy(i):
        part = pl.ds(i * chunk, chunk)
        return pltpu.make_async_copy(p_hbm.at[part], p_ref.at[part], p_sems.at[i])

    serve_copy = pltpu.make_async_copy(serve_hbm, serve_ref, serve_sem)
    for i in range(CHUNKS):
        chunk_copy(i).start()
    serve_copy.start()

    def relayout(i, carry):
        first = p_ref[i, pl.ds(0, HALF, stride=2), :]
        second = p_ref[i, pl.ds(1, HALF, stride=2), :]
        turned = pltpu.roll(jnp.where(mask, second, first), B, 1)
        own[i, pl.ds(0, HALF, stride=2), :] = jnp.where(mask, first, turned)
        own[i, pl.ds(1, HALF, stride=2), :] = jnp.where(mask, turned, second)
        return carry

    for i in range(CHUNKS):
        chunk_copy(i).wait()
        lax.fori_loop(i * chunk, (i + 1) * chunk, relayout, 0, unroll=4)
    serve_copy.wait()
    me = me_ref[0]

    targets = n // CHUNKS

    def serve(target, carry):
        offset = target - me - 1
        offset = jnp.where(offset < 0, offset + n, offset)
        offset = jnp.minimum(offset, n - 2)
        for c in range(serve_count):
            send[target, c] = own[serve_ref[c, offset]]
        return carry

    def send_copy(i):
        part = pl.ds(i * targets, targets)
        return pltpu.make_async_copy(send.at[part], send_hbm.at[part], send_sems.at[i])

    for i in range(CHUNKS):
        lax.fori_loop(i * targets, (i + 1) * targets, serve, 0, unroll=4)
        send_copy(i).start()
    for i in range(CHUNKS):
        send_copy(i).wait()


def add_products(acc, out, dest):
    mask = low_lanes(HALF)
    for p in range(2):
        even, odd = out[p * B : p * B + HALF], out[p * B + HALF : (p + 1) * B]
        turned = pltpu.roll(jnp.where(mask, odd, even), B, 1)
        first, second = dest[2 * p], dest[2 * p + 1]
        left, right = jnp.where(mask, even, turned), jnp.where(mask, turned, odd)
        old_first, old_second = acc[first], acc[second]
        acc[first] = old_first + left
        acc[second] = old_second + right + jnp.where(first == second, left, 0.0)


def add_entry(acc, meta, e, lp, right_ref):
    weights = split_rows(right_ref[meta[e * META]])
    out = jnp.dot(jnp.concatenate([lp, lp], axis=1), weights, preferred_element_type=jnp.float32)
    add_products(acc, out, [meta[e * META + 1 + j] for j in range(4)])


def near_kernel(
    n, count_row, a_slot, contrib, me_ref, own_ref, a_ref, left_hbm, slots_hbm, meta_ref, acc, left_ref, turned_rows, near_meta, place_of, sems
):
    step = pl.program_id(0)
    rows = own_ref.shape[0]
    blocks = a_ref.shape[1]
    slot_count = acc.shape[0] - 1
    per_row = contrib.shape[1] // 2
    entries = rows * blocks
    last = near_meta.shape[0] - 1

    @pl.when(step == 0)
    def start():
        me = me_ref[0]

        def put(ref, at, row, i, k):
            ref[at * META] = row
            for p in range(2):
                for q in range(2):
                    ref[at * META + 1 + 2 * p + q] = contrib[i, p * per_row + 2 * k + q]

        def put_pad(ref, at):
            ref[at * META] = 0
            for j in range(4):
                ref[at * META + 1 + j] = slot_count

        def scan_row(i, carry):
            near_count, far_count = carry
            for k in range(blocks):
                slot = a_slot[k, i]
                is_near = slot < rows
                index = slot - rows
                source = me - 1 - index // 2
                source = jnp.where(source < 0, source + n, source)
                put(near_meta, near_count, jnp.where(is_near, slot, 0), i, k)
                put(meta_ref, far_count, jnp.where(is_near, 0, source * 2 + index % 2), i, k)
                place_of[i * blocks + k] = jnp.where(is_near, entries - 1 - near_count, far_count)
                near_count = near_count + jnp.where(is_near, 1, 0)
                far_count = far_count + jnp.where(is_near, 0, 1)
            return near_count, far_count

        def skip_row(i, carry):
            for k in range(blocks):
                place_of[i * blocks + k] = entries
            return carry

        live = jnp.minimum(count_row[0], rows)
        near_count, far_count = lax.fori_loop(0, live, scan_row, (0, 0))
        lax.fori_loop(live, rows, skip_row, 0)
        for j in range(UNROLL):
            put_pad(near_meta, near_count + j)
            put_pad(meta_ref, far_count + j)
        near_meta[last] = near_count
        meta_ref[last] = far_count
        acc[...] = jnp.zeros_like(acc)

    mask = low_lanes(HALF)
    y_even = own_ref[step, pl.ds(0, HALF, stride=2), :]
    y_odd = own_ref[step, pl.ds(1, HALF, stride=2), :]
    p_rows = jnp.concatenate([y_even, y_odd], axis=0)
    high = p_rows.astype(jnp.bfloat16).astype(jnp.float32)
    turned_rows[...] = jnp.concatenate([high, p_rows - high], axis=0).T
    pair = [turned_rows[pl.ds(p * B + parity, HALF, stride=2), :] for p in range(2) for parity in range(2)]
    pair = jnp.concatenate(pair, axis=0).astype(jnp.bfloat16)
    lhs = jnp.concatenate([pair, pair], axis=1)
    for k in range(blocks):
        tile = a_ref[0, k]
        turned = pltpu.roll(tile, B, 1)
        both = jnp.concatenate([jnp.where(mask, tile, turned), jnp.where(mask, turned, tile)], axis=0)
        left = jnp.dot(lhs, split_rows(both), preferred_element_type=jnp.float32)
        left_high = left.astype(jnp.bfloat16).astype(jnp.float32)
        packed = jnp.where(low_lanes(2 * B), left_high, left - left_high)
        left_ref[place_of[step * blocks + k]] = packed.astype(jnp.bfloat16)

    @pl.when(step == pl.num_programs(0) - 1)
    def own_products():
        left_copy = pltpu.make_async_copy(left_ref, left_hbm, sems.at[0])
        left_copy.start()

        def products(g, carry):
            for u in range(UNROLL):
                e = g * UNROLL + u
                add_entry(acc, near_meta, e, left_ref[jnp.maximum(entries - 1 - e, 0)], own_ref)
            return carry

        lax.fori_loop(0, (near_meta[last] + UNROLL - 1) // UNROLL, products, 0)

        slots_copy = pltpu.make_async_copy(acc.at[pl.ds(0, slot_count)], slots_hbm, sems.at[1])
        slots_copy.start()
        left_copy.wait()
        slots_copy.wait()


def far_kernel(n, cap, me_ref, meta, left_hbm, recv, near_hbm, *refs):
    groups = n // GROUP
    steps, _, rest_steps = split_steps(groups)
    outs = PLACES + len(rest_steps)
    far_slots, rest_slots = refs[:PLACES], dict(zip(rest_steps, refs[PLACES:outs]))
    own_mine, own_other, acc, near, ring, ring_sems, near_sem = refs[outs:]
    me = me_ref[0]
    count = meta[meta.shape[0] - 1]
    turns = (count + UNROLL - 1) // UNROLL

    per_turn = UNROLL // FETCH

    def left_copy(i):
        buffer = lax.rem(i, DEPTH)
        return pltpu.make_async_copy(left_hbm.at[pl.ds(i * FETCH, FETCH)], ring.at[buffer], ring_sems.at[buffer])

    def fetch(g):
        @pl.when(g < turns)
        def go():
            for i in range(per_turn):
                left_copy(g * per_turn + i).start()

    ahead = DEPTH // per_turn - 1
    for g in range(ahead):
        fetch(g)
    acc[...] = jnp.zeros_like(acc)
    near_copy = pltpu.make_async_copy(near_hbm, near, near_sem)
    near_copy.start()

    def products(g, carry):
        fetch(g + ahead)
        for i in range(per_turn):
            left_copy(g * per_turn + i).wait()
        for u in range(UNROLL):
            buffer = lax.rem(g * per_turn + u // FETCH, DEPTH)
            add_entry(acc, meta, g * UNROLL + u, ring[buffer, u % FETCH], recv)
        return carry

    lax.fori_loop(0, turns, products, 0)
    near_copy.wait()
    place = lax.rem(me // 2, PLACES)
    group = me // GROUP

    core = lax.rem(me, 2)

    def packed(j, step, side):
        at = group + step
        at = jnp.where(at >= groups, at - groups, at)
        m = at * GROUP + (place ^ j) * 2 + side - me
        m = jnp.where(m < 0, m + n, m)
        return [acc[m * cap + c] + near[m * cap + c] for c in range(cap)]

    for j in range(PLACES):
        for other in range(2):
            side = 1 - core if other else core
            for step, (first, count) in steps.items():
                for c, slot in enumerate(packed(j, step, side)):
                    far_slots[j][side, c, first : first + count] = slot[:count]
                    if step in rest_slots:
                        rest_slots[step][other, j, c] = slot[count:]
            for c, slot in enumerate(packed(j, 0, side)):
                (own_other if other else own_mine)[j, c] = slot


def add_slots(target, table, entry, m, slots, rows=None, from_rows=None):
    rows = pl.ds(0, HALF) if rows is None else rows
    for c in range(slots.shape[0]):
        value = slots[c] if from_rows is None else slots[c, from_rows]
        target[table[entry * slots.shape[0] + c, m], rows, :] += value


def combine_far_kernel(n, me_ref, table, *refs):
    slots, (mine, other) = refs[:PLACES], refs[PLACES:]
    groups = n // GROUP
    me = me_ref[0]
    core = lax.rem(me, 2)
    place = lax.rem(me // 2, PLACES)
    group = me // GROUP

    steps, _, _ = split_steps(groups)
    for target in (mine, other):
        target[...] = jnp.zeros_like(target)
    for step, (first, count) in steps.items():
        part = pl.ds(first, count)
        at = group + step
        at = jnp.where(at >= groups, at - groups, at)
        for target, side in ((mine, core), (other, 1 - core)):
            for j in range(PLACES):
                m = (at - group) * GROUP + (place - (place ^ j)) * 2 + side - core
                m = jnp.where(m < 0, m + n, m)
                add_slots(target, table, (at ^ group) * 2 + (side ^ core), m, slots[j].at[side], part, part)


def combine_own_kernel(n, me_ref, table, mine, got, rest_got, *refs):
    rest_mine, tiles = refs[:-PLACES], refs[-PLACES:]
    me = me_ref[0]
    core = lax.rem(me, 2)
    place = lax.rem(me // 2, PLACES)
    for j in range(PLACES):
        tiles[j][...] = jnp.zeros_like(tiles[j])
        for other in range(2):
            m = ((place ^ j) - place) * 2 + other * (2 * core - 1)
            m = jnp.where(m < 0, m + n, m)
            add_slots(tiles[j], table, j, m, (got if other else mine).at[j])
            for index, step in enumerate(split_steps(n // GROUP)[2]):
                at = m + step * GROUP
                at = jnp.where(at >= n, at - n, at)
                rest = rest_got.at[index, j] if other else rest_mine[index].at[0, j]
                add_slots(tiles[j], table, j, at, rest, pl.ds(HALF - REST, REST))


def final_kernel(*refs):
    own, far, out_ref, total = refs[:PLACES], refs[PLACES:-2], refs[-2], refs[-1]
    for t in range(TO):
        total[t * HALF : (t + 1) * HALF] = own[0][t] + own[1][t] + own[2][t] + own[3][t]
        for part in far:
            total[t * HALF : t * HALF + part.shape[1]] += part[t]
    for r in range(HALF):
        out_ref[:, r * LANES : (r + 1) * LANES] = total[pl.ds(r, TO, stride=HALF), :]


def spec(space):
    return pl.BlockSpec(memory_space=space)


def body(a_blocks, p_blocks, a_slot, serve_rows, row_count, contrib_slot, recv_tile):
    n = lax.axis_size("elem")
    rows, blocks, _ = a_blocks.shape
    cap = recv_tile.shape[2]
    serve_count = serve_rows.shape[2]
    f32, i32, bf16 = jnp.float32, jnp.int32, jnp.bfloat16
    smem, vmem, hbm = spec(pltpu.SMEM), spec(pltpu.VMEM), spec(pl.ANY)
    pinned = n <= 32
    me = lax.axis_index("elem").astype(i32).reshape(1)

    def shape(dims, dtype):
        return pltpu.VMEM(dims, dtype) if pinned else jax.ShapeDtypeStruct(dims, dtype)

    def pin(value):
        return pltpu.with_memory_space_constraint(value, pltpu.VMEM) if pinned else value

    def pin_hbm(value):
        return pltpu.with_memory_space_constraint(value, pltpu.HBM)

    def across(value, partner):
        return lax.ppermute(value, "elem", [(i, partner(i)) for i in range(n)])

    p_view = p_blocks.reshape(rows, 2, HALF, LANES).transpose(0, 2, 1, 3).reshape(rows, B, LANES)
    own, send = pl.pallas_call(
        functools.partial(prep_kernel, n),
        out_shape=(shape((rows, B, LANES), f32), pltpu.HBM((n, serve_count, B, LANES), f32)),
        in_specs=[smem, hbm, hbm],
        out_specs=(vmem, hbm),
        scratch_shapes=[
            pltpu.VMEM((rows, B, LANES), f32),
            pltpu.VMEM((n, serve_count, B, LANES), f32),
            pltpu.SMEM((serve_count, n - 1), i32),
            pltpu.SemaphoreType.DMA((CHUNKS,)),
            pltpu.SemaphoreType.DMA,
            pltpu.SemaphoreType.DMA((CHUNKS,)),
        ],
        compiler_params=params(8 + n // 8),
        name="prep",
    )(me, pin_hbm(serve_rows[0].T), pin_hbm(p_view))

    recv = lax.all_to_all(
        send.reshape(n, serve_count * B, LANES), "elem", split_axis=0, concat_axis=0, tiled=True
    ).reshape(n * serve_count, B, LANES)

    groups = n // GROUP
    table = recv_tile.transpose(0, 2, 1)
    own_table = jnp.concatenate([table] + [across(table, lambda i, j=j: i ^ (2 * j)) for j in range(1, PLACES)], axis=0)
    pair = jnp.concatenate([table, across(table, lambda i: i ^ 1)], axis=0)
    a_blocks, pair = lax.optimization_barrier((a_blocks, pair))
    far_table = jnp.concatenate(
        [pair] + [across(pair, lambda i, step=step: i ^ (step * GROUP)) for step in range(1, groups)], axis=0
    )
    recv, own_table, far_table = lax.optimization_barrier((recv, own_table, far_table))
    own_table, far_table = own_table.reshape(-1, n), far_table.reshape(-1, n)

    entries = rows * blocks
    slot_count = n * cap
    meta_size = (entries + 2 * UNROLL) * META
    a_tiles = a_blocks.reshape(rows, blocks, HALF, LANES)
    left, near_slots, meta = pl.pallas_call(
        functools.partial(near_kernel, n),
        grid=(rows,),
        out_shape=(
            pltpu.HBM((entries + UNROLL, 2 * B, LANES), bf16),
            pltpu.HBM((slot_count, HALF, LANES), f32),
            jax.ShapeDtypeStruct((meta_size,), i32),
        ),
        in_specs=[smem, smem, smem, smem, vmem, pl.BlockSpec((1, blocks, HALF, LANES), lambda i: (i, 0, 0, 0))],
        out_specs=(hbm, hbm, smem),
        scratch_shapes=[
            pltpu.VMEM((slot_count + 1, HALF, LANES), f32),
            pltpu.VMEM((entries + UNROLL, 2 * B, LANES), bf16),
            pltpu.VMEM((2 * B, LANES), f32),
            pltpu.SMEM((meta_size,), i32),
            pltpu.SMEM((entries,), i32),
            pltpu.SemaphoreType.DMA((2,)),
        ],
        compiler_params=params(20 + n // 4, dimension_semantics=("arbitrary",)),
        cost_estimate=pl.CostEstimate(flops=8 * entries * 2 * B * LANES * LANES, bytes_accessed=16 << 20, transcendentals=0),
        name="near",
    )(row_count, a_slot.T, contrib_slot, me, pin(own), a_tiles)

    steps, far_rows, rest_steps = split_steps(groups)
    slot_shapes = [shape((2, cap, far_rows, LANES), f32)] * PLACES
    slot_shapes += [shape((2, PLACES, cap, REST, LANES), f32)] * len(rest_steps)
    slot_shapes += [shape((PLACES, cap, HALF, LANES), f32)] * 2
    slots = pl.pallas_call(
        functools.partial(far_kernel, n, cap),
        out_shape=slot_shapes,
        in_specs=[smem, smem, hbm, vmem, hbm],
        out_specs=[vmem] * len(slot_shapes),
        scratch_shapes=[
            pltpu.VMEM((slot_count + 1, HALF, LANES), f32),
            pltpu.VMEM((slot_count, HALF, LANES), f32),
            pltpu.VMEM((DEPTH, FETCH, 2 * B, LANES), bf16),
            pltpu.SemaphoreType.DMA((DEPTH,)),
            pltpu.SemaphoreType.DMA,
        ],
        compiler_params=params(16 + n // 4),
        cost_estimate=pl.CostEstimate(flops=4 * entries * 2 * B * LANES * LANES, bytes_accessed=16 << 20, transcendentals=0),
        name="far",
    )(me, meta, pin_hbm(left), pin(recv), pin_hbm(near_slots))

    def combine(kernel, out_shape, table, parts):
        return pl.pallas_call(
            functools.partial(kernel, n),
            out_shape=out_shape,
            in_specs=[smem, smem] + [vmem] * len(parts),
            out_specs=[vmem] * len(out_shape),
            compiler_params=params(8 + n // 4),
            name=kernel.__name__,
        )(me, table, *[pin(part) for part in parts])

    def in_group(values):
        return [values[0]] + [across(values[j], lambda i, j=j: i ^ (2 * j)) for j in range(1, PLACES)]

    def over_groups(values):
        return [across(value, lambda i, step=step: (i + step * GROUP) % n) for step, value in values]

    def other_core(value):
        return across(value, lambda i: i ^ 1)

    own_mine, own_other = slots[-2:]
    rest = over_groups(zip(rest_steps, slots[PLACES:-2]))
    far_slots = in_group(slots[:PLACES])
    rest_got = other_core(jnp.stack([part[1] for part in rest]))
    own_shape = [shape((TO, HALF, LANES), f32)] * PLACES
    own_tiles = combine(combine_own_kernel, own_shape, own_table, [own_mine, other_core(own_other), rest_got] + rest)
    far_shape = [shape((TO, far_rows, LANES), f32)] * 2
    mine, other = combine(combine_far_kernel, far_shape, far_table, far_slots)
    got = other_core(other)
    summed = [mine[:, first : first + count] + got[:, first : first + count] for first, count in steps.values()]
    summed, own_tiles = lax.optimization_barrier((summed, own_tiles))
    far_parts = over_groups(zip(steps, summed))
    parts = in_group(own_tiles) + far_parts

    return pl.pallas_call(
        final_kernel,
        out_shape=jax.ShapeDtypeStruct((TO, B * B), f32),
        in_specs=[vmem] * len(parts),
        out_specs=vmem,
        scratch_shapes=[pltpu.VMEM((TO * HALF, LANES), f32)],
        compiler_params=params(8),
        name="final",
    )(*[pin(part) for part in parts])


def solution(mesh):
    in_specs = (
        P("elem", None, None),
        P("elem", None, None),
        P("elem", None),
        P("elem", None, None),
        P("elem"),
        P("elem", None),
        P("elem", None, None),
    )
    out_specs = P("elem", None)
    return jax.shard_map(body, mesh=mesh, in_specs=in_specs, out_specs=out_specs, check_vma=False)
```

```python
import functools

import jax
import jax.numpy as jnp
from jax import lax
from jax.experimental import pallas as pl
from jax.experimental.pallas import tpu as pltpu
from jax.sharding import PartitionSpec as P

B = 64
HALF = B // 2
LANES = 2 * B
TO = 8
PLACES = 4
GROUP = 2 * PLACES
CHUNKS = 4
REST = HALF // 2
FETCH = 16
DEPTH = 6
UNROLL = 32
META = 8
MIB = 1 << 20


def low_lanes(rows):
    return lax.broadcasted_iota(jnp.int32, (rows, LANES), 1) < B


def split_rows(value):
    high = value.astype(jnp.bfloat16)
    low = (value - high.astype(jnp.float32)).astype(jnp.bfloat16)
    return jnp.concatenate([high, high, low, low], axis=0)


def split_steps(groups):
    steps, first = {}, 0
    for step in range(1, groups):
        rows = HALF if step == groups // 2 else HALF - REST
        steps[step] = first, rows
        first += rows
    return steps, first, [step for step, (_, rows) in steps.items() if rows < HALF]


def params(mib, **more):
    return pltpu.CompilerParams(vmem_limit_bytes=mib * MIB, **more)


def prep_kernel(n, me_ref, serve_hbm, p_hbm, own, send_hbm, p_ref, send, serve_ref, p_sems, serve_sem, send_sems):
    rows = p_ref.shape[0]
    serve_count = serve_ref.shape[0]
    mask = low_lanes(HALF)
    chunk = rows // CHUNKS

    def chunk_copy(i):
        part = pl.ds(i * chunk, chunk)
        return pltpu.make_async_copy(p_hbm.at[part], p_ref.at[part], p_sems.at[i])

    serve_copy = pltpu.make_async_copy(serve_hbm, serve_ref, serve_sem)
    for i in range(CHUNKS):
        chunk_copy(i).start()
    serve_copy.start()

    def relayout(i, carry):
        first = p_ref[i, pl.ds(0, HALF, stride=2), :]
        second = p_ref[i, pl.ds(1, HALF, stride=2), :]
        turned = pltpu.roll(jnp.where(mask, second, first), B, 1)
        own[i, pl.ds(0, HALF, stride=2), :] = jnp.where(mask, first, turned)
        own[i, pl.ds(1, HALF, stride=2), :] = jnp.where(mask, turned, second)
        return carry

    for i in range(CHUNKS):
        chunk_copy(i).wait()
        lax.fori_loop(i * chunk, (i + 1) * chunk, relayout, 0, unroll=4)
    serve_copy.wait()
    me = me_ref[0]

    targets = n // CHUNKS

    def serve(target, carry):
        offset = target - me - 1
        offset = jnp.where(offset < 0, offset + n, offset)
        offset = jnp.minimum(offset, n - 2)
        for c in range(serve_count):
            send[target, c] = own[serve_ref[c, offset]]
        return carry

    def send_copy(i):
        part = pl.ds(i * targets, targets)
        return pltpu.make_async_copy(send.at[part], send_hbm.at[part], send_sems.at[i])

    for i in range(CHUNKS):
        lax.fori_loop(i * targets, (i + 1) * targets, serve, 0, unroll=4)
        send_copy(i).start()
    for i in range(CHUNKS):
        send_copy(i).wait()


def add_products(acc, out, dest):
    mask = low_lanes(HALF)
    for p in range(2):
        even, odd = out[p * B : p * B + HALF], out[p * B + HALF : (p + 1) * B]
        turned = pltpu.roll(jnp.where(mask, odd, even), B, 1)
        first, second = dest[2 * p], dest[2 * p + 1]
        left, right = jnp.where(mask, even, turned), jnp.where(mask, turned, odd)
        old_first, old_second = acc[first], acc[second]
        acc[first] = old_first + left
        acc[second] = old_second + right + jnp.where(first == second, left, 0.0)


def add_entry(acc, meta, e, lp, right_ref):
    weights = split_rows(right_ref[meta[e * META]])
    out = jnp.dot(jnp.concatenate([lp, lp], axis=1), weights, preferred_element_type=jnp.float32)
    add_products(acc, out, [meta[e * META + 1 + j] for j in range(4)])


def near_kernel(
    n, count_row, a_slot, contrib, me_ref, own_ref, a_ref, left_hbm, slots_hbm, meta_ref, acc, left_ref, turned_rows, near_meta, place_of, sems
):
    step = pl.program_id(0)
    rows = own_ref.shape[0]
    blocks = a_ref.shape[1]
    slot_count = acc.shape[0] - 1
    per_row = contrib.shape[1] // 2
    entries = rows * blocks
    last = near_meta.shape[0] - 1

    @pl.when(step == 0)
    def start():
        me = me_ref[0]

        def put(ref, at, row, i, k):
            ref[at * META] = row
            for p in range(2):
                for q in range(2):
                    ref[at * META + 1 + 2 * p + q] = contrib[i, p * per_row + 2 * k + q]

        def put_pad(ref, at):
            ref[at * META] = 0
            for j in range(4):
                ref[at * META + 1 + j] = slot_count

        def scan_row(i, carry):
            near_count, far_count = carry
            for k in range(blocks):
                slot = a_slot[k, i]
                is_near = slot < rows
                index = slot - rows
                source = me - 1 - index // 2
                source = jnp.where(source < 0, source + n, source)
                put(near_meta, near_count, jnp.where(is_near, slot, 0), i, k)
                put(meta_ref, far_count, jnp.where(is_near, 0, source * 2 + index % 2), i, k)
                place_of[i * blocks + k] = jnp.where(is_near, entries - 1 - near_count, far_count)
                near_count = near_count + jnp.where(is_near, 1, 0)
                far_count = far_count + jnp.where(is_near, 0, 1)
            return near_count, far_count

        def skip_row(i, carry):
            for k in range(blocks):
                place_of[i * blocks + k] = entries
            return carry

        live = jnp.minimum(count_row[0], rows)
        near_count, far_count = lax.fori_loop(0, live, scan_row, (0, 0))
        lax.fori_loop(live, rows, skip_row, 0)
        for j in range(UNROLL):
            put_pad(near_meta, near_count + j)
            put_pad(meta_ref, far_count + j)
        near_meta[last] = near_count
        meta_ref[last] = far_count
        acc[...] = jnp.zeros_like(acc)

    mask = low_lanes(HALF)
    y_even = own_ref[step, pl.ds(0, HALF, stride=2), :]
    y_odd = own_ref[step, pl.ds(1, HALF, stride=2), :]
    p_rows = jnp.concatenate([y_even, y_odd], axis=0)
    high = p_rows.astype(jnp.bfloat16).astype(jnp.float32)
    turned_rows[...] = jnp.concatenate([high, p_rows - high], axis=0).T
    pair = [turned_rows[pl.ds(p * B + parity, HALF, stride=2), :] for p in range(2) for parity in range(2)]
    pair = jnp.concatenate(pair, axis=0).astype(jnp.bfloat16)
    lhs = jnp.concatenate([pair, pair], axis=1)
    for k in range(blocks):
        tile = a_ref[0, k]
        turned = pltpu.roll(tile, B, 1)
        both = jnp.concatenate([jnp.where(mask, tile, turned), jnp.where(mask, turned, tile)], axis=0)
        left = jnp.dot(lhs, split_rows(both), preferred_element_type=jnp.float32)
        left_high = left.astype(jnp.bfloat16).astype(jnp.float32)
        packed = jnp.where(low_lanes(2 * B), left_high, left - left_high)
        left_ref[place_of[step * blocks + k]] = packed.astype(jnp.bfloat16)

    @pl.when(step == pl.num_programs(0) - 1)
    def own_products():
        left_copy = pltpu.make_async_copy(left_ref, left_hbm, sems.at[0])
        left_copy.start()

        def products(g, carry):
            for u in range(UNROLL):
                e = g * UNROLL + u
                add_entry(acc, near_meta, e, left_ref[jnp.maximum(entries - 1 - e, 0)], own_ref)
            return carry

        lax.fori_loop(0, (near_meta[last] + UNROLL - 1) // UNROLL, products, 0)

        slots_copy = pltpu.make_async_copy(acc.at[pl.ds(0, slot_count)], slots_hbm, sems.at[1])
        slots_copy.start()
        left_copy.wait()
        slots_copy.wait()


def far_kernel(n, cap, me_ref, meta, left_hbm, recv, near_hbm, *refs):
    groups = n // GROUP
    steps, _, rest_steps = split_steps(groups)
    outs = PLACES + len(rest_steps)
    far_slots, rest_slots = refs[:PLACES], dict(zip(rest_steps, refs[PLACES:outs]))
    own_mine, own_other, acc, near, ring, ring_sems, near_sem = refs[outs:]
    me = me_ref[0]
    count = meta[meta.shape[0] - 1]
    turns = (count + UNROLL - 1) // UNROLL

    per_turn = UNROLL // FETCH

    def left_copy(i):
        buffer = lax.rem(i, DEPTH)
        return pltpu.make_async_copy(left_hbm.at[pl.ds(i * FETCH, FETCH)], ring.at[buffer], ring_sems.at[buffer])

    def fetch(g):
        @pl.when(g < turns)
        def go():
            for i in range(per_turn):
                left_copy(g * per_turn + i).start()

    ahead = DEPTH // per_turn - 1
    for g in range(ahead):
        fetch(g)
    acc[...] = jnp.zeros_like(acc)
    near_copy = pltpu.make_async_copy(near_hbm, near, near_sem)
    near_copy.start()

    def products(g, carry):
        fetch(g + ahead)
        for i in range(per_turn):
            left_copy(g * per_turn + i).wait()
        for u in range(UNROLL):
            buffer = lax.rem(g * per_turn + u // FETCH, DEPTH)
            add_entry(acc, meta, g * UNROLL + u, ring[buffer, u % FETCH], recv)
        return carry

    lax.fori_loop(0, turns, products, 0)
    near_copy.wait()
    place = lax.rem(me // 2, PLACES)
    group = me // GROUP

    core = lax.rem(me, 2)

    def packed(j, step, side):
        at = group + step
        at = jnp.where(at >= groups, at - groups, at)
        m = at * GROUP + (place ^ j) * 2 + side - me
        m = jnp.where(m < 0, m + n, m)
        return [acc[m * cap + c] + near[m * cap + c] for c in range(cap)]

    for j in range(PLACES):
        for other in range(2):
            side = 1 - core if other else core
            for step, (first, count) in steps.items():
                for c, slot in enumerate(packed(j, step, side)):
                    far_slots[j][side, c, first : first + count] = slot[:count]
                    if step in rest_slots:
                        rest_slots[step][other, j, c] = slot[count:]
            for c, slot in enumerate(packed(j, 0, side)):
                (own_other if other else own_mine)[j, c] = slot


def add_slots(target, table, entry, m, slots, rows=None, from_rows=None):
    rows = pl.ds(0, HALF) if rows is None else rows
    for c in range(slots.shape[0]):
        value = slots[c] if from_rows is None else slots[c, from_rows]
        target[table[entry * slots.shape[0] + c, m], rows, :] += value


def combine_far_kernel(n, me_ref, table, *refs):
    slots, (mine, other) = refs[:PLACES], refs[PLACES:]
    groups = n // GROUP
    me = me_ref[0]
    core = lax.rem(me, 2)
    place = lax.rem(me // 2, PLACES)
    group = me // GROUP

    steps, _, _ = split_steps(groups)
    for target in (mine, other):
        target[...] = jnp.zeros_like(target)
    for step, (first, count) in steps.items():
        part = pl.ds(first, count)
        at = group + step
        at = jnp.where(at >= groups, at - groups, at)
        for target, side in ((mine, core), (other, 1 - core)):
            for j in range(PLACES):
                m = (at - group) * GROUP + (place - (place ^ j)) * 2 + side - core
                m = jnp.where(m < 0, m + n, m)
                add_slots(target, table, (at ^ group) * 2 + (side ^ core), m, slots[j].at[side], part, part)


def combine_own_kernel(n, me_ref, table, mine, got, rest_got, *refs):
    rest_mine, tiles = refs[:-PLACES], refs[-PLACES:]
    me = me_ref[0]
    core = lax.rem(me, 2)
    place = lax.rem(me // 2, PLACES)
    for j in range(PLACES):
        tiles[j][...] = jnp.zeros_like(tiles[j])
        for other in range(2):
            m = ((place ^ j) - place) * 2 + other * (2 * core - 1)
            m = jnp.where(m < 0, m + n, m)
            add_slots(tiles[j], table, j, m, (got if other else mine).at[j])
            for index, step in enumerate(split_steps(n // GROUP)[2]):
                at = m + step * GROUP
                at = jnp.where(at >= n, at - n, at)
                rest = rest_got.at[index, j] if other else rest_mine[index].at[0, j]
                add_slots(tiles[j], table, j, at, rest, pl.ds(HALF - REST, REST))


def final_kernel(*refs):
    far, own, out_ref, total = refs[: -2 - PLACES], refs[-2 - PLACES : -2], refs[-2], refs[-1]
    for t in range(TO):
        total[t * HALF : (t + 1) * HALF] = own[0][t] + own[1][t] + own[2][t] + own[3][t]
        for part in far:
            total[t * HALF : t * HALF + part.shape[1]] += part[t]
    for r in range(HALF):
        out_ref[:, r * LANES : (r + 1) * LANES] = total[pl.ds(r, TO, stride=HALF), :]


def spec(space):
    return pl.BlockSpec(memory_space=space)


def body(a_blocks, p_blocks, a_slot, serve_rows, row_count, contrib_slot, recv_tile):
    n = lax.axis_size("elem")
    rows, blocks, _ = a_blocks.shape
    cap = recv_tile.shape[2]
    serve_count = serve_rows.shape[2]
    f32, i32, bf16 = jnp.float32, jnp.int32, jnp.bfloat16
    smem, vmem, hbm = spec(pltpu.SMEM), spec(pltpu.VMEM), spec(pl.ANY)
    pinned = n <= 32
    me = lax.axis_index("elem").astype(i32).reshape(1)

    def shape(dims, dtype):
        return pltpu.VMEM(dims, dtype) if pinned else jax.ShapeDtypeStruct(dims, dtype)

    def pin(value):
        return pltpu.with_memory_space_constraint(value, pltpu.VMEM) if pinned else value

    def pin_hbm(value):
        return pltpu.with_memory_space_constraint(value, pltpu.HBM)

    def across(value, partner):
        return lax.ppermute(value, "elem", [(i, partner(i)) for i in range(n)])

    p_view = p_blocks.reshape(rows, 2, HALF, LANES).transpose(0, 2, 1, 3).reshape(rows, B, LANES)
    own, send = pl.pallas_call(
        functools.partial(prep_kernel, n),
        out_shape=(shape((rows, B, LANES), f32), pltpu.HBM((n, serve_count, B, LANES), f32)),
        in_specs=[smem, hbm, hbm],
        out_specs=(vmem, hbm),
        scratch_shapes=[
            pltpu.VMEM((rows, B, LANES), f32),
            pltpu.VMEM((n, serve_count, B, LANES), f32),
            pltpu.SMEM((serve_count, n - 1), i32),
            pltpu.SemaphoreType.DMA((CHUNKS,)),
            pltpu.SemaphoreType.DMA,
            pltpu.SemaphoreType.DMA((CHUNKS,)),
        ],
        compiler_params=params(8 + n // 8),
        name="prep",
    )(me, pin_hbm(serve_rows[0].T), pin_hbm(p_view))

    recv = lax.all_to_all(
        send.reshape(n, serve_count * B, LANES), "elem", split_axis=0, concat_axis=0, tiled=True
    ).reshape(n * serve_count, B, LANES)

    groups = n // GROUP
    table = recv_tile.transpose(0, 2, 1)
    own_table = jnp.concatenate([table] + [across(table, lambda i, j=j: i ^ (2 * j)) for j in range(1, PLACES)], axis=0)
    pair = jnp.concatenate([table, across(table, lambda i: i ^ 1)], axis=0)
    a_blocks, pair = lax.optimization_barrier((a_blocks, pair))
    far_table = jnp.concatenate(
        [pair] + [across(pair, lambda i, step=step: i ^ (step * GROUP)) for step in range(1, groups)], axis=0
    )
    recv, own_table, far_table = lax.optimization_barrier((recv, own_table, far_table))
    own_table, far_table = own_table.reshape(-1, n), far_table.reshape(-1, n)

    entries = rows * blocks
    slot_count = n * cap
    meta_size = (entries + 2 * UNROLL) * META
    a_tiles = a_blocks.reshape(rows, blocks, HALF, LANES)
    left, near_slots, meta = pl.pallas_call(
        functools.partial(near_kernel, n),
        grid=(rows,),
        out_shape=(
            pltpu.HBM((entries + UNROLL, 2 * B, LANES), bf16),
            pltpu.HBM((slot_count, HALF, LANES), f32),
            jax.ShapeDtypeStruct((meta_size,), i32),
        ),
        in_specs=[smem, smem, smem, smem, vmem, pl.BlockSpec((1, blocks, HALF, LANES), lambda i: (i, 0, 0, 0))],
        out_specs=(hbm, hbm, smem),
        scratch_shapes=[
            pltpu.VMEM((slot_count + 1, HALF, LANES), f32),
            pltpu.VMEM((entries + UNROLL, 2 * B, LANES), bf16),
            pltpu.VMEM((2 * B, LANES), f32),
            pltpu.SMEM((meta_size,), i32),
            pltpu.SMEM((entries,), i32),
            pltpu.SemaphoreType.DMA((2,)),
        ],
        compiler_params=params(20 + n // 4, dimension_semantics=("arbitrary",)),
        cost_estimate=pl.CostEstimate(flops=8 * entries * 2 * B * LANES * LANES, bytes_accessed=16 << 20, transcendentals=0),
        name="near",
    )(row_count, a_slot.T, contrib_slot, me, pin(own), a_tiles)

    steps, far_rows, rest_steps = split_steps(groups)
    slot_shapes = [shape((2, cap, far_rows, LANES), f32)] * PLACES
    slot_shapes += [shape((2, PLACES, cap, REST, LANES), f32)] * len(rest_steps)
    slot_shapes += [shape((PLACES, cap, HALF, LANES), f32)] * 2
    slots = pl.pallas_call(
        functools.partial(far_kernel, n, cap),
        out_shape=slot_shapes,
        in_specs=[smem, smem, hbm, vmem, hbm],
        out_specs=[vmem] * len(slot_shapes),
        scratch_shapes=[
            pltpu.VMEM((slot_count + 1, HALF, LANES), f32),
            pltpu.VMEM((slot_count, HALF, LANES), f32),
            pltpu.VMEM((DEPTH, FETCH, 2 * B, LANES), bf16),
            pltpu.SemaphoreType.DMA((DEPTH,)),
            pltpu.SemaphoreType.DMA,
        ],
        compiler_params=params(16 + n // 4),
        cost_estimate=pl.CostEstimate(flops=4 * entries * 2 * B * LANES * LANES, bytes_accessed=16 << 20, transcendentals=0),
        name="far",
    )(me, meta, pin_hbm(left), pin(recv), pin_hbm(near_slots))

    def combine(kernel, out_shape, table, parts):
        return pl.pallas_call(
            functools.partial(kernel, n),
            out_shape=out_shape,
            in_specs=[smem, smem] + [vmem] * len(parts),
            out_specs=[vmem] * len(out_shape),
            compiler_params=params(8 + n // 4),
            name=kernel.__name__,
        )(me, table, *[pin(part) for part in parts])

    def in_group(values):
        return [values[0]] + [across(values[j], lambda i, j=j: i ^ (2 * j)) for j in range(1, PLACES)]

    def over_groups(values):
        return [across(value, lambda i, step=step: (i + step * GROUP) % n) for step, value in values]

    def other_core(value):
        return across(value, lambda i: i ^ 1)

    own_mine, own_other = slots[-2:]
    rest = over_groups(zip(rest_steps, slots[PLACES:-2]))
    far_slots = in_group(slots[:PLACES])
    rest_got = other_core(jnp.stack([part[1] for part in rest]))
    own_shape = [shape((TO, HALF, LANES), f32)] * PLACES
    own_tiles = combine(combine_own_kernel, own_shape, own_table, [own_mine, other_core(own_other), rest_got] + rest)
    far_shape = [shape((TO, far_rows, LANES), f32)] * 2
    mine, other = combine(combine_far_kernel, far_shape, far_table, far_slots)
    got = other_core(other)
    summed = [mine[:, first : first + count] + got[:, first : first + count] for first, count in steps.values()]
    order = sorted(zip(steps, summed), key=lambda item: abs(item[0] - groups // 2) * 2 - (item[0] > groups // 2))
    far_parts = over_groups(order)
    parts = far_parts + in_group(own_tiles)

    return pl.pallas_call(
        final_kernel,
        out_shape=jax.ShapeDtypeStruct((TO, B * B), f32),
        in_specs=[vmem] * len(parts),
        out_specs=vmem,
        scratch_shapes=[pltpu.VMEM((TO * HALF, LANES), f32)],
        compiler_params=params(8),
        name="final",
    )(*[pin(part) for part in parts])


def solution(mesh):
    in_specs = (
        P("elem", None, None),
        P("elem", None, None),
        P("elem", None),
        P("elem", None, None),
        P("elem"),
        P("elem", None),
        P("elem", None, None),
    )
    out_specs = P("elem", None)
    return jax.shard_map(body, mesh=mesh, in_specs=in_specs, out_specs=out_specs, check_vma=False)
```

```python
import functools

import jax
import jax.numpy as jnp
from jax import lax
from jax.experimental import pallas as pl
from jax.experimental.pallas import tpu as pltpu
from jax.sharding import PartitionSpec as P

B = 64
HALF = B // 2
LANES = 2 * B
TO = 8
PLACES = 4
GROUP = 2 * PLACES
CHUNKS = 4
REST = HALF // 2
FETCH = 16
DEPTH = 8
UNROLL = 32
META = 8
MIB = 1 << 20


def low_lanes(rows):
    return lax.broadcasted_iota(jnp.int32, (rows, LANES), 1) < B


def split_rows(value):
    high = value.astype(jnp.bfloat16)
    low = (value - high.astype(jnp.float32)).astype(jnp.bfloat16)
    return jnp.concatenate([high, high, low, low], axis=0)


def split_steps(groups):
    steps, first = {}, 0
    for step in range(1, groups):
        rows = HALF if step == groups // 2 else HALF - REST
        steps[step] = first, rows
        first += rows
    return steps, first, [step for step, (_, rows) in steps.items() if rows < HALF]


def params(mib, **more):
    return pltpu.CompilerParams(vmem_limit_bytes=mib * MIB, **more)


def prep_kernel(n, me_ref, serve_hbm, p_hbm, own, send_hbm, p_ref, send, serve_ref, p_sems, serve_sem, send_sems):
    rows = p_ref.shape[0]
    serve_count = serve_ref.shape[0]
    mask = low_lanes(HALF)
    chunk = rows // CHUNKS

    def chunk_copy(i):
        part = pl.ds(i * chunk, chunk)
        return pltpu.make_async_copy(p_hbm.at[part], p_ref.at[part], p_sems.at[i])

    serve_copy = pltpu.make_async_copy(serve_hbm, serve_ref, serve_sem)
    for i in range(CHUNKS):
        chunk_copy(i).start()
    serve_copy.start()

    def relayout(i, carry):
        first = p_ref[i, pl.ds(0, HALF, stride=2), :]
        second = p_ref[i, pl.ds(1, HALF, stride=2), :]
        turned = pltpu.roll(jnp.where(mask, second, first), B, 1)
        own[i, pl.ds(0, HALF, stride=2), :] = jnp.where(mask, first, turned)
        own[i, pl.ds(1, HALF, stride=2), :] = jnp.where(mask, turned, second)
        return carry

    for i in range(CHUNKS):
        chunk_copy(i).wait()
        lax.fori_loop(i * chunk, (i + 1) * chunk, relayout, 0, unroll=4)
    serve_copy.wait()
    me = me_ref[0]

    targets = n // CHUNKS

    def serve(target, carry):
        offset = target - me - 1
        offset = jnp.where(offset < 0, offset + n, offset)
        offset = jnp.minimum(offset, n - 2)
        for c in range(serve_count):
            send[target, c] = own[serve_ref[c, offset]]
        return carry

    def send_copy(i):
        part = pl.ds(i * targets, targets)
        return pltpu.make_async_copy(send.at[part], send_hbm.at[part], send_sems.at[i])

    for i in range(CHUNKS):
        lax.fori_loop(i * targets, (i + 1) * targets, serve, 0, unroll=4)
        send_copy(i).start()
    for i in range(CHUNKS):
        send_copy(i).wait()


def add_products(acc, out, dest):
    mask = low_lanes(HALF)
    for p in range(2):
        even, odd = out[p * B : p * B + HALF], out[p * B + HALF : (p + 1) * B]
        turned = pltpu.roll(jnp.where(mask, odd, even), B, 1)
        first, second = dest[2 * p], dest[2 * p + 1]
        left, right = jnp.where(mask, even, turned), jnp.where(mask, turned, odd)
        old_first, old_second = acc[first], acc[second]
        acc[first] = old_first + left
        acc[second] = old_second + right + jnp.where(first == second, left, 0.0)


def add_entry(acc, meta, e, lp, right_ref):
    weights = split_rows(right_ref[meta[e * META]])
    out = jnp.dot(jnp.concatenate([lp, lp], axis=1), weights, preferred_element_type=jnp.float32)
    add_products(acc, out, [meta[e * META + 1 + j] for j in range(4)])


def near_kernel(
    n, count_row, a_slot, contrib, me_ref, own_ref, a_ref, left_hbm, slots_hbm, meta_ref, acc, left_ref, turned_rows, near_meta, place_of, sems
):
    step = pl.program_id(0)
    rows = own_ref.shape[0]
    blocks = a_ref.shape[1]
    slot_count = acc.shape[0] - 1
    per_row = contrib.shape[1] // 2
    entries = rows * blocks
    last = near_meta.shape[0] - 1

    @pl.when(step == 0)
    def start():
        me = me_ref[0]

        def put(ref, at, row, i, k):
            ref[at * META] = row
            for p in range(2):
                for q in range(2):
                    ref[at * META + 1 + 2 * p + q] = contrib[i, p * per_row + 2 * k + q]

        def put_pad(ref, at):
            ref[at * META] = 0
            for j in range(4):
                ref[at * META + 1 + j] = slot_count

        def scan_row(i, carry):
            near_count, far_count = carry
            for k in range(blocks):
                slot = a_slot[k, i]
                is_near = slot < rows
                index = slot - rows
                source = me - 1 - index // 2
                source = jnp.where(source < 0, source + n, source)
                put(near_meta, near_count, jnp.where(is_near, slot, 0), i, k)
                put(meta_ref, far_count, jnp.where(is_near, 0, source * 2 + index % 2), i, k)
                place_of[i * blocks + k] = jnp.where(is_near, entries - 1 - near_count, far_count)
                near_count = near_count + jnp.where(is_near, 1, 0)
                far_count = far_count + jnp.where(is_near, 0, 1)
            return near_count, far_count

        def skip_row(i, carry):
            for k in range(blocks):
                place_of[i * blocks + k] = entries
            return carry

        live = jnp.minimum(count_row[0], rows)
        near_count, far_count = lax.fori_loop(0, live, scan_row, (0, 0))
        lax.fori_loop(live, rows, skip_row, 0)
        for j in range(UNROLL):
            put_pad(near_meta, near_count + j)
            put_pad(meta_ref, far_count + j)
        near_meta[last] = near_count
        meta_ref[last] = far_count
        acc[...] = jnp.zeros_like(acc)

    mask = low_lanes(HALF)
    y_even = own_ref[step, pl.ds(0, HALF, stride=2), :]
    y_odd = own_ref[step, pl.ds(1, HALF, stride=2), :]
    p_rows = jnp.concatenate([y_even, y_odd], axis=0)
    high = p_rows.astype(jnp.bfloat16).astype(jnp.float32)
    turned_rows[...] = jnp.concatenate([high, p_rows - high], axis=0).T
    pair = [turned_rows[pl.ds(p * B + parity, HALF, stride=2), :] for p in range(2) for parity in range(2)]
    pair = jnp.concatenate(pair, axis=0).astype(jnp.bfloat16)
    lhs = jnp.concatenate([pair, pair], axis=1)
    for k in range(blocks):
        tile = a_ref[0, k]
        turned = pltpu.roll(tile, B, 1)
        both = jnp.concatenate([jnp.where(mask, tile, turned), jnp.where(mask, turned, tile)], axis=0)
        left = jnp.dot(lhs, split_rows(both), preferred_element_type=jnp.float32)
        left_high = left.astype(jnp.bfloat16).astype(jnp.float32)
        packed = jnp.where(low_lanes(2 * B), left_high, left - left_high)
        left_ref[place_of[step * blocks + k]] = packed.astype(jnp.bfloat16)

    @pl.when(step == pl.num_programs(0) - 1)
    def own_products():
        left_copy = pltpu.make_async_copy(left_ref, left_hbm, sems.at[0])
        left_copy.start()

        def products(g, carry):
            for u in range(UNROLL):
                e = g * UNROLL + u
                add_entry(acc, near_meta, e, left_ref[jnp.maximum(entries - 1 - e, 0)], own_ref)
            return carry

        lax.fori_loop(0, (near_meta[last] + UNROLL - 1) // UNROLL, products, 0)

        slots_copy = pltpu.make_async_copy(acc.at[pl.ds(0, slot_count)], slots_hbm, sems.at[1])
        slots_copy.start()
        left_copy.wait()
        slots_copy.wait()


def far_kernel(n, cap, me_ref, meta, left_hbm, recv, near_hbm, *refs):
    groups = n // GROUP
    steps, _, rest_steps = split_steps(groups)
    outs = PLACES + len(rest_steps)
    far_slots, rest_slots = refs[:PLACES], dict(zip(rest_steps, refs[PLACES:outs]))
    own_mine, own_other, acc, near, ring, ring_sems, near_sem = refs[outs:]
    me = me_ref[0]
    count = meta[meta.shape[0] - 1]
    turns = (count + UNROLL - 1) // UNROLL

    per_turn = UNROLL // FETCH

    def left_copy(i):
        buffer = lax.rem(i, DEPTH)
        return pltpu.make_async_copy(left_hbm.at[pl.ds(i * FETCH, FETCH)], ring.at[buffer], ring_sems.at[buffer])

    def fetch(g):
        @pl.when(g < turns)
        def go():
            for i in range(per_turn):
                left_copy(g * per_turn + i).start()

    ahead = DEPTH // per_turn - 1
    for g in range(ahead):
        fetch(g)
    acc[...] = jnp.zeros_like(acc)
    near_copy = pltpu.make_async_copy(near_hbm, near, near_sem)
    near_copy.start()

    def products(g, carry):
        fetch(g + ahead)
        for i in range(per_turn):
            left_copy(g * per_turn + i).wait()
        for u in range(UNROLL):
            buffer = lax.rem(g * per_turn + u // FETCH, DEPTH)
            add_entry(acc, meta, g * UNROLL + u, ring[buffer, u % FETCH], recv)
        return carry

    lax.fori_loop(0, turns, products, 0)
    near_copy.wait()
    place = lax.rem(me // 2, PLACES)
    group = me // GROUP

    core = lax.rem(me, 2)

    def packed(j, step, side):
        at = group + step
        at = jnp.where(at >= groups, at - groups, at)
        m = at * GROUP + (place ^ j) * 2 + side - me
        m = jnp.where(m < 0, m + n, m)
        return [acc[m * cap + c] + near[m * cap + c] for c in range(cap)]

    for j in range(PLACES):
        for other in range(2):
            side = 1 - core if other else core
            for step, (first, count) in steps.items():
                for c, slot in enumerate(packed(j, step, side)):
                    far_slots[j][side, c, first : first + count] = slot[:count]
                    if step in rest_slots:
                        rest_slots[step][other, j, c] = slot[count:]
            for c, slot in enumerate(packed(j, 0, side)):
                (own_other if other else own_mine)[j, c] = slot


def add_slots(target, table, entry, m, slots, rows=None, from_rows=None):
    rows = pl.ds(0, HALF) if rows is None else rows
    for c in range(slots.shape[0]):
        value = slots[c] if from_rows is None else slots[c, from_rows]
        target[table[entry * slots.shape[0] + c, m], rows, :] += value


def combine_far_kernel(n, me_ref, table, *refs):
    slots, (mine, other) = refs[:PLACES], refs[PLACES:]
    groups = n // GROUP
    me = me_ref[0]
    core = lax.rem(me, 2)
    place = lax.rem(me // 2, PLACES)
    group = me // GROUP

    steps, _, _ = split_steps(groups)
    for target in (mine, other):
        target[...] = jnp.zeros_like(target)
    for step, (first, count) in steps.items():
        part = pl.ds(first, count)
        at = group + step
        at = jnp.where(at >= groups, at - groups, at)
        for target, side in ((mine, core), (other, 1 - core)):
            for j in range(PLACES):
                m = (at - group) * GROUP + (place - (place ^ j)) * 2 + side - core
                m = jnp.where(m < 0, m + n, m)
                add_slots(target, table, (at ^ group) * 2 + (side ^ core), m, slots[j].at[side], part, part)


def combine_own_kernel(n, me_ref, table, mine, got, rest_got, *refs):
    rest_mine, tiles = refs[:-PLACES], refs[-PLACES:]
    me = me_ref[0]
    core = lax.rem(me, 2)
    place = lax.rem(me // 2, PLACES)
    for j in range(PLACES):
        tiles[j][...] = jnp.zeros_like(tiles[j])
        for other in range(2):
            m = ((place ^ j) - place) * 2 + other * (2 * core - 1)
            m = jnp.where(m < 0, m + n, m)
            add_slots(tiles[j], table, j, m, (got if other else mine).at[j])
            for index, step in enumerate(split_steps(n // GROUP)[2]):
                at = m + step * GROUP
                at = jnp.where(at >= n, at - n, at)
                rest = rest_got.at[index, j] if other else rest_mine[index].at[0, j]
                add_slots(tiles[j], table, j, at, rest, pl.ds(HALF - REST, REST))


def final_kernel(*refs):
    far, own, out_ref, total = refs[: -2 - PLACES], refs[-2 - PLACES : -2], refs[-2], refs[-1]
    for t in range(TO):
        total[t * HALF : (t + 1) * HALF] = own[0][t] + own[1][t] + own[2][t] + own[3][t]
        for part in far:
            total[t * HALF : t * HALF + part.shape[1]] += part[t]
    for r in range(HALF):
        out_ref[:, r * LANES : (r + 1) * LANES] = total[pl.ds(r, TO, stride=HALF), :]


def spec(space):
    return pl.BlockSpec(memory_space=space)


def body(a_blocks, p_blocks, a_slot, serve_rows, row_count, contrib_slot, recv_tile):
    n = lax.axis_size("elem")
    rows, blocks, _ = a_blocks.shape
    cap = recv_tile.shape[2]
    serve_count = serve_rows.shape[2]
    f32, i32, bf16 = jnp.float32, jnp.int32, jnp.bfloat16
    smem, vmem, hbm = spec(pltpu.SMEM), spec(pltpu.VMEM), spec(pl.ANY)
    pinned = n <= 32
    me = lax.axis_index("elem").astype(i32).reshape(1)

    def shape(dims, dtype):
        return pltpu.VMEM(dims, dtype) if pinned else jax.ShapeDtypeStruct(dims, dtype)

    def pin(value):
        return pltpu.with_memory_space_constraint(value, pltpu.VMEM) if pinned else value

    def pin_hbm(value):
        return pltpu.with_memory_space_constraint(value, pltpu.HBM)

    def across(value, partner):
        return lax.ppermute(value, "elem", [(i, partner(i)) for i in range(n)])

    p_view = p_blocks.reshape(rows, 2, HALF, LANES).transpose(0, 2, 1, 3).reshape(rows, B, LANES)
    own, send = pl.pallas_call(
        functools.partial(prep_kernel, n),
        out_shape=(shape((rows, B, LANES), f32), pltpu.HBM((n, serve_count, B, LANES), f32)),
        in_specs=[smem, hbm, hbm],
        out_specs=(vmem, hbm),
        scratch_shapes=[
            pltpu.VMEM((rows, B, LANES), f32),
            pltpu.VMEM((n, serve_count, B, LANES), f32),
            pltpu.SMEM((serve_count, n - 1), i32),
            pltpu.SemaphoreType.DMA((CHUNKS,)),
            pltpu.SemaphoreType.DMA,
            pltpu.SemaphoreType.DMA((CHUNKS,)),
        ],
        compiler_params=params(8 + n // 8),
        name="prep",
    )(me, pin_hbm(serve_rows[0].T), pin_hbm(p_view))

    recv = lax.all_to_all(
        send.reshape(n, serve_count * B, LANES), "elem", split_axis=0, concat_axis=0, tiled=True
    ).reshape(n * serve_count, B, LANES)

    groups = n // GROUP
    table = recv_tile.transpose(0, 2, 1)
    own_table = jnp.concatenate([table] + [across(table, lambda i, j=j: i ^ (2 * j)) for j in range(1, PLACES)], axis=0)
    pair = jnp.concatenate([table, across(table, lambda i: i ^ 1)], axis=0)
    a_blocks, pair = lax.optimization_barrier((a_blocks, pair))
    far_table = jnp.concatenate(
        [pair] + [across(pair, lambda i, step=step: i ^ (step * GROUP)) for step in range(1, groups)], axis=0
    )
    recv, own_table, far_table = lax.optimization_barrier((recv, own_table, far_table))
    own_table, far_table = own_table.reshape(-1, n), far_table.reshape(-1, n)

    entries = rows * blocks
    slot_count = n * cap
    meta_size = (entries + 2 * UNROLL) * META
    a_tiles = a_blocks.reshape(rows, blocks, HALF, LANES)
    left, near_slots, meta = pl.pallas_call(
        functools.partial(near_kernel, n),
        grid=(rows,),
        out_shape=(
            pltpu.HBM((entries + UNROLL, 2 * B, LANES), bf16),
            pltpu.HBM((slot_count, HALF, LANES), f32),
            jax.ShapeDtypeStruct((meta_size,), i32),
        ),
        in_specs=[smem, smem, smem, smem, vmem, pl.BlockSpec((1, blocks, HALF, LANES), lambda i: (i, 0, 0, 0))],
        out_specs=(hbm, hbm, smem),
        scratch_shapes=[
            pltpu.VMEM((slot_count + 1, HALF, LANES), f32),
            pltpu.VMEM((entries + UNROLL, 2 * B, LANES), bf16),
            pltpu.VMEM((2 * B, LANES), f32),
            pltpu.SMEM((meta_size,), i32),
            pltpu.SMEM((entries,), i32),
            pltpu.SemaphoreType.DMA((2,)),
        ],
        compiler_params=params(20 + n // 4, dimension_semantics=("arbitrary",)),
        cost_estimate=pl.CostEstimate(flops=8 * entries * 2 * B * LANES * LANES, bytes_accessed=16 << 20, transcendentals=0),
        name="near",
    )(row_count, a_slot.T, contrib_slot, me, pin(own), a_tiles)

    steps, far_rows, rest_steps = split_steps(groups)
    slot_shapes = [shape((2, cap, far_rows, LANES), f32)] * PLACES
    slot_shapes += [shape((2, PLACES, cap, REST, LANES), f32)] * len(rest_steps)
    slot_shapes += [shape((PLACES, cap, HALF, LANES), f32)] * 2
    slots = pl.pallas_call(
        functools.partial(far_kernel, n, cap),
        out_shape=slot_shapes,
        in_specs=[smem, smem, hbm, vmem, hbm],
        out_specs=[vmem] * len(slot_shapes),
        scratch_shapes=[
            pltpu.VMEM((slot_count + 1, HALF, LANES), f32),
            pltpu.VMEM((slot_count, HALF, LANES), f32),
            pltpu.VMEM((DEPTH, FETCH, 2 * B, LANES), bf16),
            pltpu.SemaphoreType.DMA((DEPTH,)),
            pltpu.SemaphoreType.DMA,
        ],
        compiler_params=params(16 + n // 4),
        cost_estimate=pl.CostEstimate(flops=4 * entries * 2 * B * LANES * LANES, bytes_accessed=16 << 20, transcendentals=0),
        name="far",
    )(me, meta, pin_hbm(left), pin(recv), pin_hbm(near_slots))

    def combine(kernel, out_shape, table, parts):
        return pl.pallas_call(
            functools.partial(kernel, n),
            out_shape=out_shape,
            in_specs=[smem, smem] + [vmem] * len(parts),
            out_specs=[vmem] * len(out_shape),
            compiler_params=params(8 + n // 4),
            name=kernel.__name__,
        )(me, table, *[pin(part) for part in parts])

    def in_group(values):
        return [values[0]] + [across(values[j], lambda i, j=j: i ^ (2 * j)) for j in range(1, PLACES)]

    def over_groups(values):
        return [across(value, lambda i, step=step: (i + step * GROUP) % n) for step, value in values]

    def other_core(value):
        return across(value, lambda i: i ^ 1)

    own_mine, own_other = slots[-2:]
    rest = over_groups(zip(rest_steps, slots[PLACES:-2]))
    far_slots = in_group(slots[:PLACES])
    rest_got = other_core(jnp.stack([part[1] for part in rest]))
    own_shape = [shape((TO, HALF, LANES), f32)] * PLACES
    own_tiles = combine(combine_own_kernel, own_shape, own_table, [own_mine, other_core(own_other), rest_got] + rest)
    far_shape = [shape((TO, far_rows, LANES), f32)] * 2
    mine, other = combine(combine_far_kernel, far_shape, far_table, far_slots)
    got = other_core(other)
    summed = [mine[:, first : first + count] + got[:, first : first + count] for first, count in steps.values()]
    order = sorted(zip(steps, summed), key=lambda item: abs(item[0] - groups // 2) * 2 - (item[0] > groups // 2))
    far_parts = over_groups(order)
    parts = far_parts + in_group(own_tiles)

    return pl.pallas_call(
        final_kernel,
        out_shape=jax.ShapeDtypeStruct((TO, B * B), f32),
        in_specs=[vmem] * len(parts),
        out_specs=vmem,
        scratch_shapes=[pltpu.VMEM((TO * HALF, LANES), f32)],
        compiler_params=params(8),
        name="final",
    )(*[pin(part) for part in parts])


def solution(mesh):
    in_specs = (
        P("elem", None, None),
        P("elem", None, None),
        P("elem", None),
        P("elem", None, None),
        P("elem"),
        P("elem", None),
        P("elem", None, None),
    )
    out_specs = P("elem", None)
    return jax.shard_map(body, mesh=mesh, in_specs=in_specs, out_specs=out_specs, check_vma=False)
```

```python
import functools

import jax
import jax.numpy as jnp
from jax import lax
from jax.experimental import pallas as pl
from jax.experimental.pallas import tpu as pltpu
from jax.sharding import PartitionSpec as P

B = 64
HALF = B // 2
LANES = 2 * B
TO = 8
PLACES = 4
GROUP = 2 * PLACES
CHUNKS = 4
REST = HALF // 2
FETCH = 16
DEPTH = 8
UNROLL = 32
META = 8
MIB = 1 << 20


def low_lanes(rows):
    return lax.broadcasted_iota(jnp.int32, (rows, LANES), 1) < B


def split_rows(value):
    high = value.astype(jnp.bfloat16)
    low = (value - high.astype(jnp.float32)).astype(jnp.bfloat16)
    return jnp.concatenate([high, high, low, low], axis=0)


def split_steps(groups):
    steps, first = {}, 0
    for step in range(1, groups):
        rows = HALF if step == groups // 2 else HALF - REST
        steps[step] = first, rows
        first += rows
    return steps, first, [step for step, (_, rows) in steps.items() if rows < HALF]


def params(mib, **more):
    return pltpu.CompilerParams(vmem_limit_bytes=mib * MIB, **more)


def prep_kernel(n, me_ref, serve_hbm, p_hbm, own, send_hbm, p_ref, send, serve_ref, p_sems, serve_sem, send_sems):
    rows = p_ref.shape[0]
    serve_count = serve_ref.shape[0]
    mask = low_lanes(HALF)
    chunk = rows // CHUNKS

    def chunk_copy(i):
        part = pl.ds(i * chunk, chunk)
        return pltpu.make_async_copy(p_hbm.at[part], p_ref.at[part], p_sems.at[i])

    serve_copy = pltpu.make_async_copy(serve_hbm, serve_ref, serve_sem)
    for i in range(CHUNKS):
        chunk_copy(i).start()
    serve_copy.start()

    def relayout(i, carry):
        first = p_ref[i, pl.ds(0, HALF, stride=2), :]
        second = p_ref[i, pl.ds(1, HALF, stride=2), :]
        turned = pltpu.roll(jnp.where(mask, second, first), B, 1)
        own[i, pl.ds(0, HALF, stride=2), :] = jnp.where(mask, first, turned)
        own[i, pl.ds(1, HALF, stride=2), :] = jnp.where(mask, turned, second)
        return carry

    for i in range(CHUNKS):
        chunk_copy(i).wait()
        lax.fori_loop(i * chunk, (i + 1) * chunk, relayout, 0, unroll=4)
    serve_copy.wait()
    me = me_ref[0]

    targets = n // CHUNKS

    def serve(target, carry):
        offset = target - me - 1
        offset = jnp.where(offset < 0, offset + n, offset)
        offset = jnp.minimum(offset, n - 2)
        for c in range(serve_count):
            send[target, c] = own[serve_ref[c, offset]]
        return carry

    def send_copy(i):
        part = pl.ds(i * targets, targets)
        return pltpu.make_async_copy(send.at[part], send_hbm.at[part], send_sems.at[i])

    for i in range(CHUNKS):
        lax.fori_loop(i * targets, (i + 1) * targets, serve, 0, unroll=4)
        send_copy(i).start()
    for i in range(CHUNKS):
        send_copy(i).wait()


def add_products(acc, out, dest):
    mask = low_lanes(HALF)
    for p in range(2):
        even, odd = out[p * B : p * B + HALF], out[p * B + HALF : (p + 1) * B]
        turned = pltpu.roll(jnp.where(mask, odd, even), B, 1)
        first, second = dest[2 * p], dest[2 * p + 1]
        left, right = jnp.where(mask, even, turned), jnp.where(mask, turned, odd)
        old_first, old_second = acc[first], acc[second]
        acc[first] = old_first + left
        acc[second] = old_second + right + jnp.where(first == second, left, 0.0)


def add_entry(acc, meta, e, lp, right_ref):
    weights = split_rows(right_ref[meta[e * META]])
    out = jnp.dot(jnp.concatenate([lp, lp], axis=1), weights, preferred_element_type=jnp.float32)
    add_products(acc, out, [meta[e * META + 1 + j] for j in range(4)])


def near_kernel(
    n, count_row, a_slot, contrib, me_ref, own_ref, a_ref, left_hbm, slots_hbm, meta_ref, acc, left_ref, turned_rows, near_meta, place_of, sems
):
    step = pl.program_id(0)
    rows = own_ref.shape[0]
    blocks = a_ref.shape[1]
    slot_count = acc.shape[0] - 1
    per_row = contrib.shape[1] // 2
    entries = rows * blocks
    last = near_meta.shape[0] - 1

    @pl.when(step == 0)
    def start():
        me = me_ref[0]

        def put(ref, at, row, i, k):
            ref[at * META] = row
            for p in range(2):
                for q in range(2):
                    ref[at * META + 1 + 2 * p + q] = contrib[i, p * per_row + 2 * k + q]

        def put_pad(ref, at):
            ref[at * META] = 0
            for j in range(4):
                ref[at * META + 1 + j] = slot_count

        def scan_row(i, carry):
            near_count, far_count = carry
            for k in range(blocks):
                slot = a_slot[k, i]
                is_near = slot < rows
                index = slot - rows
                source = me - 1 - index // 2
                source = jnp.where(source < 0, source + n, source)
                put(near_meta, near_count, jnp.where(is_near, slot, 0), i, k)
                put(meta_ref, far_count, jnp.where(is_near, 0, source * 2 + index % 2), i, k)
                place_of[i * blocks + k] = jnp.where(is_near, entries - 1 - near_count, far_count)
                near_count = near_count + jnp.where(is_near, 1, 0)
                far_count = far_count + jnp.where(is_near, 0, 1)
            return near_count, far_count

        def skip_row(i, carry):
            for k in range(blocks):
                place_of[i * blocks + k] = entries
            return carry

        live = jnp.minimum(count_row[0], rows)
        near_count, far_count = lax.fori_loop(0, live, scan_row, (0, 0))
        lax.fori_loop(live, rows, skip_row, 0)
        for j in range(UNROLL):
            put_pad(near_meta, near_count + j)
            put_pad(meta_ref, far_count + j)
        near_meta[last] = near_count
        meta_ref[last] = far_count
        acc[...] = jnp.zeros_like(acc)

    mask = low_lanes(HALF)
    y_even = own_ref[step, pl.ds(0, HALF, stride=2), :]
    y_odd = own_ref[step, pl.ds(1, HALF, stride=2), :]
    p_rows = jnp.concatenate([y_even, y_odd], axis=0)
    high = p_rows.astype(jnp.bfloat16).astype(jnp.float32)
    turned_rows[...] = jnp.concatenate([high, p_rows - high], axis=0).T
    pair = [turned_rows[pl.ds(p * B + parity, HALF, stride=2), :] for p in range(2) for parity in range(2)]
    pair = jnp.concatenate(pair, axis=0).astype(jnp.bfloat16)
    lhs = jnp.concatenate([pair, pair], axis=1)
    for k in range(blocks):
        tile = a_ref[0, k]
        turned = pltpu.roll(tile, B, 1)
        both = jnp.concatenate([jnp.where(mask, tile, turned), jnp.where(mask, turned, tile)], axis=0)
        left = jnp.dot(lhs, split_rows(both), preferred_element_type=jnp.float32)
        left_high = left.astype(jnp.bfloat16).astype(jnp.float32)
        packed = jnp.where(low_lanes(2 * B), left_high, left - left_high)
        left_ref[place_of[step * blocks + k]] = packed.astype(jnp.bfloat16)

    @pl.when(step == pl.num_programs(0) - 1)
    def own_products():
        left_copy = pltpu.make_async_copy(left_ref, left_hbm, sems.at[0])
        left_copy.start()

        def products(g, carry):
            for u in range(UNROLL):
                e = g * UNROLL + u
                add_entry(acc, near_meta, e, left_ref[jnp.maximum(entries - 1 - e, 0)], own_ref)
            return carry

        lax.fori_loop(0, (near_meta[last] + UNROLL - 1) // UNROLL, products, 0)

        slots_copy = pltpu.make_async_copy(acc.at[pl.ds(0, slot_count)], slots_hbm, sems.at[1])
        slots_copy.start()
        left_copy.wait()
        slots_copy.wait()


def far_kernel(n, cap, me_ref, meta, left_hbm, recv, near_hbm, *refs):
    groups = n // GROUP
    steps, _, rest_steps = split_steps(groups)
    outs = PLACES + len(rest_steps)
    far_slots, rest_slots = refs[:PLACES], dict(zip(rest_steps, refs[PLACES:outs]))
    own_mine, own_other, acc, near, ring, ring_sems, near_sem = refs[outs:]
    me = me_ref[0]
    count = meta[meta.shape[0] - 1]
    chunks = (count + FETCH - 1) // FETCH

    per_turn = UNROLL // FETCH

    def left_copy(i):
        buffer = lax.rem(i, DEPTH)
        return pltpu.make_async_copy(left_hbm.at[pl.ds(i * FETCH, FETCH)], ring.at[buffer], ring_sems.at[buffer])

    def fetch(g):
        for i in range(per_turn):

            @pl.when(g * per_turn + i < chunks)
            def go():
                left_copy(g * per_turn + i).start()

    ahead = DEPTH // per_turn - 1
    for g in range(ahead):
        fetch(g)
    acc[...] = jnp.zeros_like(acc)
    near_copy = pltpu.make_async_copy(near_hbm, near, near_sem)
    near_copy.start()

    def products(g, carry):
        fetch(g + ahead)
        for i in range(per_turn):
            left_copy(g * per_turn + i).wait()
        for u in range(UNROLL):
            buffer = lax.rem(g * per_turn + u // FETCH, DEPTH)
            add_entry(acc, meta, g * UNROLL + u, ring[buffer, u % FETCH], recv)
        return carry

    def chunk_products(i, carry):
        left_copy(i).wait()
        for u in range(FETCH):
            add_entry(acc, meta, i * FETCH + u, ring[lax.rem(i, DEPTH), u], recv)
        return carry

    whole = count // UNROLL
    lax.fori_loop(0, whole, products, 0)
    lax.fori_loop(whole * per_turn, chunks, chunk_products, 0)
    near_copy.wait()
    place = lax.rem(me // 2, PLACES)
    group = me // GROUP

    core = lax.rem(me, 2)

    def packed(j, step, side):
        at = group + step
        at = jnp.where(at >= groups, at - groups, at)
        m = at * GROUP + (place ^ j) * 2 + side - me
        m = jnp.where(m < 0, m + n, m)
        return [acc[m * cap + c] + near[m * cap + c] for c in range(cap)]

    for j in range(PLACES):
        for other in range(2):
            side = 1 - core if other else core
            for step, (first, count) in steps.items():
                for c, slot in enumerate(packed(j, step, side)):
                    far_slots[j][side, c, first : first + count] = slot[:count]
                    if step in rest_slots:
                        rest_slots[step][other, j, c] = slot[count:]
            for c, slot in enumerate(packed(j, 0, side)):
                (own_other if other else own_mine)[j, c] = slot


def add_slots(target, table, entry, m, slots, rows=None, from_rows=None):
    rows = pl.ds(0, HALF) if rows is None else rows
    for c in range(slots.shape[0]):
        value = slots[c] if from_rows is None else slots[c, from_rows]
        target[table[entry * slots.shape[0] + c, m], rows, :] += value


def combine_far_kernel(n, me_ref, table, *refs):
    slots, (mine, other) = refs[:PLACES], refs[PLACES:]
    groups = n // GROUP
    me = me_ref[0]
    core = lax.rem(me, 2)
    place = lax.rem(me // 2, PLACES)
    group = me // GROUP

    steps, _, _ = split_steps(groups)
    for target in (mine, other):
        target[...] = jnp.zeros_like(target)
    for step, (first, count) in steps.items():
        part = pl.ds(first, count)
        at = group + step
        at = jnp.where(at >= groups, at - groups, at)
        for target, side in ((mine, core), (other, 1 - core)):
            for j in range(PLACES):
                m = (at - group) * GROUP + (place - (place ^ j)) * 2 + side - core
                m = jnp.where(m < 0, m + n, m)
                add_slots(target, table, (at ^ group) * 2 + (side ^ core), m, slots[j].at[side], part, part)


def combine_own_kernel(n, me_ref, table, mine, got, rest_got, *refs):
    rest_mine, tiles = refs[:-PLACES], refs[-PLACES:]
    me = me_ref[0]
    core = lax.rem(me, 2)
    place = lax.rem(me // 2, PLACES)
    for j in range(PLACES):
        tiles[j][...] = jnp.zeros_like(tiles[j])
        for other in range(2):
            m = ((place ^ j) - place) * 2 + other * (2 * core - 1)
            m = jnp.where(m < 0, m + n, m)
            add_slots(tiles[j], table, j, m, (got if other else mine).at[j])
            for index, step in enumerate(split_steps(n // GROUP)[2]):
                at = m + step * GROUP
                at = jnp.where(at >= n, at - n, at)
                rest = rest_got.at[index, j] if other else rest_mine[index].at[0, j]
                add_slots(tiles[j], table, j, at, rest, pl.ds(HALF - REST, REST))


def final_kernel(*refs):
    far, own, out_ref, total = refs[: -2 - PLACES], refs[-2 - PLACES : -2], refs[-2], refs[-1]
    for t in range(TO):
        total[t * HALF : (t + 1) * HALF] = own[0][t] + own[1][t] + own[2][t] + own[3][t]
        for part in far:
            total[t * HALF : t * HALF + part.shape[1]] += part[t]
    for r in range(HALF):
        out_ref[:, r * LANES : (r + 1) * LANES] = total[pl.ds(r, TO, stride=HALF), :]


def spec(space):
    return pl.BlockSpec(memory_space=space)


def body(a_blocks, p_blocks, a_slot, serve_rows, row_count, contrib_slot, recv_tile):
    n = lax.axis_size("elem")
    rows, blocks, _ = a_blocks.shape
    cap = recv_tile.shape[2]
    serve_count = serve_rows.shape[2]
    f32, i32, bf16 = jnp.float32, jnp.int32, jnp.bfloat16
    smem, vmem, hbm = spec(pltpu.SMEM), spec(pltpu.VMEM), spec(pl.ANY)
    pinned = n <= 32
    me = lax.axis_index("elem").astype(i32).reshape(1)

    def shape(dims, dtype):
        return pltpu.VMEM(dims, dtype) if pinned else jax.ShapeDtypeStruct(dims, dtype)

    def pin(value):
        return pltpu.with_memory_space_constraint(value, pltpu.VMEM) if pinned else value

    def pin_hbm(value):
        return pltpu.with_memory_space_constraint(value, pltpu.HBM)

    def across(value, partner):
        return lax.ppermute(value, "elem", [(i, partner(i)) for i in range(n)])

    p_view = p_blocks.reshape(rows, 2, HALF, LANES).transpose(0, 2, 1, 3).reshape(rows, B, LANES)
    own, send = pl.pallas_call(
        functools.partial(prep_kernel, n),
        out_shape=(shape((rows, B, LANES), f32), pltpu.HBM((n, serve_count, B, LANES), f32)),
        in_specs=[smem, hbm, hbm],
        out_specs=(vmem, hbm),
        scratch_shapes=[
            pltpu.VMEM((rows, B, LANES), f32),
            pltpu.VMEM((n, serve_count, B, LANES), f32),
            pltpu.SMEM((serve_count, n - 1), i32),
            pltpu.SemaphoreType.DMA((CHUNKS,)),
            pltpu.SemaphoreType.DMA,
            pltpu.SemaphoreType.DMA((CHUNKS,)),
        ],
        compiler_params=params(8 + n // 8),
        name="prep",
    )(me, pin_hbm(serve_rows[0].T), pin_hbm(p_view))

    recv = lax.all_to_all(
        send.reshape(n, serve_count * B, LANES), "elem", split_axis=0, concat_axis=0, tiled=True
    ).reshape(n * serve_count, B, LANES)

    groups = n // GROUP
    table = recv_tile.transpose(0, 2, 1)
    own_table = jnp.concatenate([table] + [across(table, lambda i, j=j: i ^ (2 * j)) for j in range(1, PLACES)], axis=0)
    pair = jnp.concatenate([table, across(table, lambda i: i ^ 1)], axis=0)
    a_blocks, pair = lax.optimization_barrier((a_blocks, pair))
    far_table = jnp.concatenate(
        [pair] + [across(pair, lambda i, step=step: i ^ (step * GROUP)) for step in range(1, groups)], axis=0
    )
    recv, own_table, far_table = lax.optimization_barrier((recv, own_table, far_table))
    own_table, far_table = own_table.reshape(-1, n), far_table.reshape(-1, n)

    entries = rows * blocks
    slot_count = n * cap
    meta_size = (entries + 2 * UNROLL) * META
    a_tiles = a_blocks.reshape(rows, blocks, HALF, LANES)
    left, near_slots, meta = pl.pallas_call(
        functools.partial(near_kernel, n),
        grid=(rows,),
        out_shape=(
            pltpu.HBM((entries + UNROLL, 2 * B, LANES), bf16),
            pltpu.HBM((slot_count, HALF, LANES), f32),
            jax.ShapeDtypeStruct((meta_size,), i32),
        ),
        in_specs=[smem, smem, smem, smem, vmem, pl.BlockSpec((1, blocks, HALF, LANES), lambda i: (i, 0, 0, 0))],
        out_specs=(hbm, hbm, smem),
        scratch_shapes=[
            pltpu.VMEM((slot_count + 1, HALF, LANES), f32),
            pltpu.VMEM((entries + UNROLL, 2 * B, LANES), bf16),
            pltpu.VMEM((2 * B, LANES), f32),
            pltpu.SMEM((meta_size,), i32),
            pltpu.SMEM((entries,), i32),
            pltpu.SemaphoreType.DMA((2,)),
        ],
        compiler_params=params(20 + n // 4, dimension_semantics=("arbitrary",)),
        cost_estimate=pl.CostEstimate(flops=8 * entries * 2 * B * LANES * LANES, bytes_accessed=16 << 20, transcendentals=0),
        name="near",
    )(row_count, a_slot.T, contrib_slot, me, pin(own), a_tiles)

    steps, far_rows, rest_steps = split_steps(groups)
    slot_shapes = [shape((2, cap, far_rows, LANES), f32)] * PLACES
    slot_shapes += [shape((2, PLACES, cap, REST, LANES), f32)] * len(rest_steps)
    slot_shapes += [shape((PLACES, cap, HALF, LANES), f32)] * 2
    slots = pl.pallas_call(
        functools.partial(far_kernel, n, cap),
        out_shape=slot_shapes,
        in_specs=[smem, smem, hbm, vmem, hbm],
        out_specs=[vmem] * len(slot_shapes),
        scratch_shapes=[
            pltpu.VMEM((slot_count + 1, HALF, LANES), f32),
            pltpu.VMEM((slot_count, HALF, LANES), f32),
            pltpu.VMEM((DEPTH, FETCH, 2 * B, LANES), bf16),
            pltpu.SemaphoreType.DMA((DEPTH,)),
            pltpu.SemaphoreType.DMA,
        ],
        compiler_params=params(16 + n // 4),
        cost_estimate=pl.CostEstimate(flops=4 * entries * 2 * B * LANES * LANES, bytes_accessed=16 << 20, transcendentals=0),
        name="far",
    )(me, meta, pin_hbm(left), pin(recv), pin_hbm(near_slots))

    def combine(kernel, out_shape, table, parts):
        return pl.pallas_call(
            functools.partial(kernel, n),
            out_shape=out_shape,
            in_specs=[smem, smem] + [vmem] * len(parts),
            out_specs=[vmem] * len(out_shape),
            compiler_params=params(8 + n // 4),
            name=kernel.__name__,
        )(me, table, *[pin(part) for part in parts])

    def in_group(values):
        return [values[0]] + [across(values[j], lambda i, j=j: i ^ (2 * j)) for j in range(1, PLACES)]

    def over_groups(values):
        return [across(value, lambda i, step=step: (i + step * GROUP) % n) for step, value in values]

    def other_core(value):
        return across(value, lambda i: i ^ 1)

    own_mine, own_other = slots[-2:]
    rest = over_groups(zip(rest_steps, slots[PLACES:-2]))
    far_slots = in_group(slots[:PLACES])
    rest_got = other_core(jnp.stack([part[1] for part in rest]))
    own_shape = [shape((TO, HALF, LANES), f32)] * PLACES
    own_tiles = combine(combine_own_kernel, own_shape, own_table, [own_mine, other_core(own_other), rest_got] + rest)
    far_shape = [shape((TO, far_rows, LANES), f32)] * 2
    mine, other = combine(combine_far_kernel, far_shape, far_table, far_slots)
    got = other_core(other)
    summed = [mine[:, first : first + count] + got[:, first : first + count] for first, count in steps.values()]
    order = sorted(zip(steps, summed), key=lambda item: abs(item[0] - groups // 2) * 2 - (item[0] > groups // 2))
    far_parts = over_groups(order)
    parts = far_parts + in_group(own_tiles)

    return pl.pallas_call(
        final_kernel,
        out_shape=jax.ShapeDtypeStruct((TO, B * B), f32),
        in_specs=[vmem] * len(parts),
        out_specs=vmem,
        scratch_shapes=[pltpu.VMEM((TO * HALF, LANES), f32)],
        compiler_params=params(8),
        name="final",
    )(*[pin(part) for part in parts])


def solution(mesh):
    in_specs = (
        P("elem", None, None),
        P("elem", None, None),
        P("elem", None),
        P("elem", None, None),
        P("elem"),
        P("elem", None),
        P("elem", None, None),
    )
    out_specs = P("elem", None)
    return jax.shard_map(body, mesh=mesh, in_specs=in_specs, out_specs=out_specs, check_vma=False)
```

```python
import functools

import jax
import jax.numpy as jnp
from jax import lax
from jax.experimental import pallas as pl
from jax.experimental.pallas import tpu as pltpu
from jax.sharding import PartitionSpec as P

B = 64
HALF = B // 2
LANES = 2 * B
TO = 8
PLACES = 4
GROUP = 2 * PLACES
CHUNKS = 4
REST = HALF // 2
FETCH = 16
DEPTH = 8
UNROLL = 32
META = 8
MIB = 1 << 20


def low_lanes(rows):
    return lax.broadcasted_iota(jnp.int32, (rows, LANES), 1) < B


def split_rows(value):
    high = value.astype(jnp.bfloat16)
    low = (value - high.astype(jnp.float32)).astype(jnp.bfloat16)
    return jnp.concatenate([high, high, low, low], axis=0)


def split_steps(groups):
    steps, first = {}, 0
    for step in range(1, groups):
        rows = HALF if step == groups // 2 else HALF - REST
        steps[step] = first, rows
        first += rows
    return steps, first, [step for step, (_, rows) in steps.items() if rows < HALF]


def params(mib, **more):
    return pltpu.CompilerParams(vmem_limit_bytes=mib * MIB, **more)


def prep_kernel(n, me_ref, serve_hbm, p_hbm, own, send_hbm, p_ref, send, serve_ref, p_sems, serve_sem, send_sems):
    rows = p_ref.shape[0]
    serve_count = serve_ref.shape[0]
    mask = low_lanes(HALF)
    chunk = rows // CHUNKS

    def chunk_copy(i):
        part = pl.ds(i * chunk, chunk)
        return pltpu.make_async_copy(p_hbm.at[part], p_ref.at[part], p_sems.at[i])

    serve_copy = pltpu.make_async_copy(serve_hbm, serve_ref, serve_sem)
    for i in range(CHUNKS):
        chunk_copy(i).start()
    serve_copy.start()

    def relayout(i, carry):
        first = p_ref[i, pl.ds(0, HALF, stride=2), :]
        second = p_ref[i, pl.ds(1, HALF, stride=2), :]
        turned = pltpu.roll(jnp.where(mask, second, first), B, 1)
        own[i, pl.ds(0, HALF, stride=2), :] = jnp.where(mask, first, turned)
        own[i, pl.ds(1, HALF, stride=2), :] = jnp.where(mask, turned, second)
        return carry

    for i in range(CHUNKS):
        chunk_copy(i).wait()
        lax.fori_loop(i * chunk, (i + 1) * chunk, relayout, 0, unroll=4)
    serve_copy.wait()
    me = me_ref[0]

    targets = n // CHUNKS

    def serve(target, carry):
        offset = target - me - 1
        offset = jnp.where(offset < 0, offset + n, offset)
        offset = jnp.minimum(offset, n - 2)
        for c in range(serve_count):
            send[target, c] = own[serve_ref[c, offset]]
        return carry

    def send_copy(i):
        part = pl.ds(i * targets, targets)
        return pltpu.make_async_copy(send.at[part], send_hbm.at[part], send_sems.at[i])

    for i in range(CHUNKS):
        lax.fori_loop(i * targets, (i + 1) * targets, serve, 0, unroll=4)
        send_copy(i).start()
    for i in range(CHUNKS):
        send_copy(i).wait()


def add_products(acc, out, dest):
    mask = low_lanes(HALF)
    for p in range(2):
        even, odd = out[p * B : p * B + HALF], out[p * B + HALF : (p + 1) * B]
        turned = pltpu.roll(jnp.where(mask, odd, even), B, 1)
        first, second = dest[2 * p], dest[2 * p + 1]
        left, right = jnp.where(mask, even, turned), jnp.where(mask, turned, odd)
        old_first, old_second = acc[first], acc[second]
        acc[first] = old_first + left
        acc[second] = old_second + right + jnp.where(first == second, left, 0.0)


def add_entry(acc, meta, e, lp, right_ref):
    weights = split_rows(right_ref[meta[e * META]])
    out = jnp.dot(jnp.concatenate([lp, lp], axis=1), weights, preferred_element_type=jnp.float32)
    add_products(acc, out, [meta[e * META + 1 + j] for j in range(4)])


def near_kernel(
    n, count_row, a_slot, contrib, me_ref, own_ref, a_ref, left_hbm, slots_hbm, meta_ref, acc, left_ref, turned_rows, near_meta, place_of, sems
):
    step = pl.program_id(0)
    rows = own_ref.shape[0]
    blocks = a_ref.shape[1]
    slot_count = acc.shape[0] - 1
    per_row = contrib.shape[1] // 2
    entries = rows * blocks
    last = near_meta.shape[0] - 1

    @pl.when(step == 0)
    def start():
        me = me_ref[0]

        def put(ref, at, row, i, k):
            ref[at * META] = row
            for p in range(2):
                for q in range(2):
                    ref[at * META + 1 + 2 * p + q] = contrib[i, p * per_row + 2 * k + q]

        def put_pad(ref, at):
            ref[at * META] = 0
            for j in range(4):
                ref[at * META + 1 + j] = slot_count

        def scan_row(i, carry):
            near_count, far_count = carry
            for k in range(blocks):
                slot = a_slot[k, i]
                is_near = slot < rows
                index = slot - rows
                source = me - 1 - index // 2
                source = jnp.where(source < 0, source + n, source)
                put(near_meta, near_count, jnp.where(is_near, slot, 0), i, k)
                put(meta_ref, far_count, jnp.where(is_near, 0, source * 2 + index % 2), i, k)
                place_of[i * blocks + k] = jnp.where(is_near, entries - 1 - near_count, far_count)
                near_count = near_count + jnp.where(is_near, 1, 0)
                far_count = far_count + jnp.where(is_near, 0, 1)
            return near_count, far_count

        def skip_row(i, carry):
            for k in range(blocks):
                place_of[i * blocks + k] = entries
            return carry

        live = jnp.minimum(count_row[0], rows)
        near_count, far_count = lax.fori_loop(0, live, scan_row, (0, 0))
        lax.fori_loop(live, rows, skip_row, 0)
        for j in range(UNROLL):
            put_pad(near_meta, near_count + j)
            put_pad(meta_ref, far_count + j)
        near_meta[last] = near_count
        meta_ref[last] = far_count
        acc[...] = jnp.zeros_like(acc)

    mask = low_lanes(HALF)
    y_even = own_ref[step, pl.ds(0, HALF, stride=2), :]
    y_odd = own_ref[step, pl.ds(1, HALF, stride=2), :]
    p_rows = jnp.concatenate([y_even, y_odd], axis=0)
    high = p_rows.astype(jnp.bfloat16).astype(jnp.float32)
    turned_rows[...] = jnp.concatenate([high, p_rows - high], axis=0).T
    pair = [turned_rows[pl.ds(p * B + parity, HALF, stride=2), :] for p in range(2) for parity in range(2)]
    pair = jnp.concatenate(pair, axis=0).astype(jnp.bfloat16)
    lhs = jnp.concatenate([pair, pair], axis=1)
    for k in range(blocks):
        tile = a_ref[0, k]
        turned = pltpu.roll(tile, B, 1)
        both = jnp.concatenate([jnp.where(mask, tile, turned), jnp.where(mask, turned, tile)], axis=0)
        left = jnp.dot(lhs, split_rows(both), preferred_element_type=jnp.float32)
        left_high = left.astype(jnp.bfloat16).astype(jnp.float32)
        packed = jnp.where(low_lanes(2 * B), left_high, left - left_high)
        left_ref[place_of[step * blocks + k]] = packed.astype(jnp.bfloat16)

    @pl.when(step == pl.num_programs(0) - 1)
    def own_products():
        left_copy = pltpu.make_async_copy(left_ref, left_hbm, sems.at[0])
        left_copy.start()

        def products(g, carry):
            for u in range(UNROLL):
                e = g * UNROLL + u
                add_entry(acc, near_meta, e, left_ref[jnp.maximum(entries - 1 - e, 0)], own_ref)
            return carry

        lax.fori_loop(0, (near_meta[last] + UNROLL - 1) // UNROLL, products, 0)

        slots_copy = pltpu.make_async_copy(acc.at[pl.ds(0, slot_count)], slots_hbm, sems.at[1])
        slots_copy.start()
        left_copy.wait()
        slots_copy.wait()


def far_kernel(n, cap, me_ref, meta, left_hbm, recv, near_hbm, *refs):
    groups = n // GROUP
    steps, _, rest_steps = split_steps(groups)
    outs = PLACES + len(rest_steps)
    far_slots, rest_slots = refs[:PLACES], dict(zip(rest_steps, refs[PLACES:outs]))
    own_mine, own_other, acc, near, ring, ring_sems, near_sem = refs[outs:]
    me = me_ref[0]
    count = meta[meta.shape[0] - 1]
    chunks = (count + FETCH - 1) // FETCH

    per_turn = UNROLL // FETCH

    def left_copy(i):
        buffer = lax.rem(i, DEPTH)
        return pltpu.make_async_copy(left_hbm.at[pl.ds(i * FETCH, FETCH)], ring.at[buffer], ring_sems.at[buffer])

    def fetch(g):
        for i in range(per_turn):

            @pl.when(g * per_turn + i < chunks)
            def go():
                left_copy(g * per_turn + i).start()

    ahead = DEPTH // per_turn - 1
    for g in range(ahead):
        fetch(g)
    acc[...] = jnp.zeros_like(acc)
    near_copy = pltpu.make_async_copy(near_hbm, near, near_sem)
    near_copy.start()

    def products(g, carry):
        fetch(g + ahead)
        for i in range(per_turn):
            left_copy(g * per_turn + i).wait()
        for u in range(UNROLL):
            buffer = lax.rem(g * per_turn + u // FETCH, DEPTH)
            add_entry(acc, meta, g * UNROLL + u, ring[buffer, u % FETCH], recv)
        return carry

    def chunk_products(i, carry):
        left_copy(i).wait()
        for u in range(FETCH):
            add_entry(acc, meta, i * FETCH + u, ring[lax.rem(i, DEPTH), u], recv)
        return carry

    whole = count // UNROLL
    lax.fori_loop(0, whole, products, 0)
    lax.fori_loop(whole * per_turn, chunks, chunk_products, 0)
    near_copy.wait()
    place = lax.rem(me // 2, PLACES)
    group = me // GROUP

    core = lax.rem(me, 2)

    def packed(j, step, side):
        at = group + step
        at = jnp.where(at >= groups, at - groups, at)
        m = at * GROUP + (place ^ j) * 2 + side - me
        m = jnp.where(m < 0, m + n, m)
        return [acc[m * cap + c] + near[m * cap + c] for c in range(cap)]

    for j in range(PLACES):
        for other in range(2):
            side = 1 - core if other else core
            for step, (first, count) in steps.items():
                for c, slot in enumerate(packed(j, step, side)):
                    far_slots[j][side, c, first : first + count] = slot[:count]
                    if step in rest_slots:
                        rest_slots[step][other, j, c] = slot[count:]
            for c, slot in enumerate(packed(j, 0, side)):
                (own_other if other else own_mine)[j, c] = slot


def add_slots(jobs):
    for c in range(max(slots.shape[0] for _, _, _, _, slots, _, _ in jobs)):
        for target, table, entry, m, slots, rows, from_rows in jobs:
            target[table[entry * slots.shape[0] + c, m], rows, :] += slots[c, from_rows]


def combine_far_kernel(n, me_ref, table, *refs):
    slots, (mine, other) = refs[:PLACES], refs[PLACES:]
    groups = n // GROUP
    me = me_ref[0]
    core = lax.rem(me, 2)
    place = lax.rem(me // 2, PLACES)
    group = me // GROUP

    steps, _, _ = split_steps(groups)
    for target in (mine, other):
        target[...] = jnp.zeros_like(target)
    for step, (first, count) in steps.items():
        part = pl.ds(first, count)
        at = group + step
        at = jnp.where(at >= groups, at - groups, at)
        for j in range(PLACES):
            jobs = []
            for target, side in ((mine, core), (other, 1 - core)):
                m = (at - group) * GROUP + (place - (place ^ j)) * 2 + side - core
                m = jnp.where(m < 0, m + n, m)
                jobs.append((target, table, (at ^ group) * 2 + (side ^ core), m, slots[j].at[side], part, part))
            add_slots(jobs)


def combine_own_kernel(n, me_ref, table, mine, got, rest_got, *refs):
    rest_mine, tiles = refs[:-PLACES], refs[-PLACES:]
    me = me_ref[0]
    core = lax.rem(me, 2)
    place = lax.rem(me // 2, PLACES)
    whole, rest_part = pl.ds(0, HALF), pl.ds(HALF - REST, REST)
    for j in range(PLACES):
        tiles[j][...] = jnp.zeros_like(tiles[j])
    for other in range(2):
        offsets = []
        for j in range(PLACES):
            m = ((place ^ j) - place) * 2 + other * (2 * core - 1)
            offsets.append(jnp.where(m < 0, m + n, m))
        slots = got if other else mine
        add_slots([(tiles[j], table, j, offsets[j], slots.at[j], whole, whole) for j in range(PLACES)])
        for index, step in enumerate(split_steps(n // GROUP)[2]):
            jobs = []
            for j in range(PLACES):
                at = offsets[j] + step * GROUP
                at = jnp.where(at >= n, at - n, at)
                rest = rest_got.at[index, j] if other else rest_mine[index].at[0, j]
                jobs.append((tiles[j], table, j, at, rest, rest_part, pl.ds(0, REST)))
            add_slots(jobs)


def final_kernel(*refs):
    far, own, out_ref, total = refs[: -2 - PLACES], refs[-2 - PLACES : -2], refs[-2], refs[-1]
    for t in range(TO):
        total[t * HALF : (t + 1) * HALF] = own[0][t] + own[1][t] + own[2][t] + own[3][t]
        for part in far:
            total[t * HALF : t * HALF + part.shape[1]] += part[t]
    for r in range(HALF):
        out_ref[:, r * LANES : (r + 1) * LANES] = total[pl.ds(r, TO, stride=HALF), :]


def spec(space):
    return pl.BlockSpec(memory_space=space)


def body(a_blocks, p_blocks, a_slot, serve_rows, row_count, contrib_slot, recv_tile):
    n = lax.axis_size("elem")
    rows, blocks, _ = a_blocks.shape
    cap = recv_tile.shape[2]
    serve_count = serve_rows.shape[2]
    f32, i32, bf16 = jnp.float32, jnp.int32, jnp.bfloat16
    smem, vmem, hbm = spec(pltpu.SMEM), spec(pltpu.VMEM), spec(pl.ANY)
    pinned = n <= 32
    me = lax.axis_index("elem").astype(i32).reshape(1)

    def shape(dims, dtype):
        return pltpu.VMEM(dims, dtype) if pinned else jax.ShapeDtypeStruct(dims, dtype)

    def pin(value):
        return pltpu.with_memory_space_constraint(value, pltpu.VMEM) if pinned else value

    def pin_hbm(value):
        return pltpu.with_memory_space_constraint(value, pltpu.HBM)

    def across(value, partner):
        return lax.ppermute(value, "elem", [(i, partner(i)) for i in range(n)])

    p_view = p_blocks.reshape(rows, 2, HALF, LANES).transpose(0, 2, 1, 3).reshape(rows, B, LANES)
    own, send = pl.pallas_call(
        functools.partial(prep_kernel, n),
        out_shape=(shape((rows, B, LANES), f32), pltpu.HBM((n, serve_count, B, LANES), f32)),
        in_specs=[smem, hbm, hbm],
        out_specs=(vmem, hbm),
        scratch_shapes=[
            pltpu.VMEM((rows, B, LANES), f32),
            pltpu.VMEM((n, serve_count, B, LANES), f32),
            pltpu.SMEM((serve_count, n - 1), i32),
            pltpu.SemaphoreType.DMA((CHUNKS,)),
            pltpu.SemaphoreType.DMA,
            pltpu.SemaphoreType.DMA((CHUNKS,)),
        ],
        compiler_params=params(8 + n // 8),
        name="prep",
    )(me, pin_hbm(serve_rows[0].T), pin_hbm(p_view))

    recv = lax.all_to_all(
        send.reshape(n, serve_count * B, LANES), "elem", split_axis=0, concat_axis=0, tiled=True
    ).reshape(n * serve_count, B, LANES)

    groups = n // GROUP
    table = recv_tile.transpose(0, 2, 1)
    own_table = jnp.concatenate([table] + [across(table, lambda i, j=j: i ^ (2 * j)) for j in range(1, PLACES)], axis=0)
    pair = jnp.concatenate([table, across(table, lambda i: i ^ 1)], axis=0)
    a_blocks, pair = lax.optimization_barrier((a_blocks, pair))
    far_table = jnp.concatenate(
        [pair] + [across(pair, lambda i, step=step: i ^ (step * GROUP)) for step in range(1, groups)], axis=0
    )
    recv, own_table, far_table = lax.optimization_barrier((recv, own_table, far_table))
    own_table, far_table = own_table.reshape(-1, n), far_table.reshape(-1, n)

    entries = rows * blocks
    slot_count = n * cap
    meta_size = (entries + 2 * UNROLL) * META
    a_tiles = a_blocks.reshape(rows, blocks, HALF, LANES)
    left, near_slots, meta = pl.pallas_call(
        functools.partial(near_kernel, n),
        grid=(rows,),
        out_shape=(
            pltpu.HBM((entries + UNROLL, 2 * B, LANES), bf16),
            pltpu.HBM((slot_count, HALF, LANES), f32),
            jax.ShapeDtypeStruct((meta_size,), i32),
        ),
        in_specs=[smem, smem, smem, smem, vmem, pl.BlockSpec((1, blocks, HALF, LANES), lambda i: (i, 0, 0, 0))],
        out_specs=(hbm, hbm, smem),
        scratch_shapes=[
            pltpu.VMEM((slot_count + 1, HALF, LANES), f32),
            pltpu.VMEM((entries + UNROLL, 2 * B, LANES), bf16),
            pltpu.VMEM((2 * B, LANES), f32),
            pltpu.SMEM((meta_size,), i32),
            pltpu.SMEM((entries,), i32),
            pltpu.SemaphoreType.DMA((2,)),
        ],
        compiler_params=params(20 + n // 4, dimension_semantics=("arbitrary",)),
        cost_estimate=pl.CostEstimate(flops=8 * entries * 2 * B * LANES * LANES, bytes_accessed=16 << 20, transcendentals=0),
        name="near",
    )(row_count, a_slot.T, contrib_slot, me, pin(own), a_tiles)

    steps, far_rows, rest_steps = split_steps(groups)
    slot_shapes = [shape((2, cap, far_rows, LANES), f32)] * PLACES
    slot_shapes += [shape((2, PLACES, cap, REST, LANES), f32)] * len(rest_steps)
    slot_shapes += [shape((PLACES, cap, HALF, LANES), f32)] * 2
    slots = pl.pallas_call(
        functools.partial(far_kernel, n, cap),
        out_shape=slot_shapes,
        in_specs=[smem, smem, hbm, vmem, hbm],
        out_specs=[vmem] * len(slot_shapes),
        scratch_shapes=[
            pltpu.VMEM((slot_count + 1, HALF, LANES), f32),
            pltpu.VMEM((slot_count, HALF, LANES), f32),
            pltpu.VMEM((DEPTH, FETCH, 2 * B, LANES), bf16),
            pltpu.SemaphoreType.DMA((DEPTH,)),
            pltpu.SemaphoreType.DMA,
        ],
        compiler_params=params(16 + n // 4),
        cost_estimate=pl.CostEstimate(flops=4 * entries * 2 * B * LANES * LANES, bytes_accessed=16 << 20, transcendentals=0),
        name="far",
    )(me, meta, pin_hbm(left), pin(recv), pin_hbm(near_slots))

    def combine(kernel, out_shape, table, parts):
        return pl.pallas_call(
            functools.partial(kernel, n),
            out_shape=out_shape,
            in_specs=[smem, smem] + [vmem] * len(parts),
            out_specs=[vmem] * len(out_shape),
            compiler_params=params(8 + n // 4),
            name=kernel.__name__,
        )(me, table, *[pin(part) for part in parts])

    def in_group(values):
        return [values[0]] + [across(values[j], lambda i, j=j: i ^ (2 * j)) for j in range(1, PLACES)]

    def over_groups(values):
        return [across(value, lambda i, step=step: (i + step * GROUP) % n) for step, value in values]

    def other_core(value):
        return across(value, lambda i: i ^ 1)

    own_mine, own_other = slots[-2:]
    rest = over_groups(zip(rest_steps, slots[PLACES:-2]))
    far_slots = in_group(slots[:PLACES])
    rest_got = other_core(jnp.stack([part[1] for part in rest]))
    own_shape = [shape((TO, HALF, LANES), f32)] * PLACES
    own_tiles = combine(combine_own_kernel, own_shape, own_table, [own_mine, other_core(own_other), rest_got] + rest)
    far_shape = [shape((TO, far_rows, LANES), f32)] * 2
    mine, other = combine(combine_far_kernel, far_shape, far_table, far_slots)
    got = other_core(other)
    summed = [mine[:, first : first + count] + got[:, first : first + count] for first, count in steps.values()]
    order = sorted(zip(steps, summed), key=lambda item: abs(item[0] - groups // 2) * 2 - (item[0] > groups // 2))
    far_parts = over_groups(order)
    parts = far_parts + in_group(own_tiles)

    return pl.pallas_call(
        final_kernel,
        out_shape=jax.ShapeDtypeStruct((TO, B * B), f32),
        in_specs=[vmem] * len(parts),
        out_specs=vmem,
        scratch_shapes=[pltpu.VMEM((TO * HALF, LANES), f32)],
        compiler_params=params(8),
        name="final",
    )(*[pin(part) for part in parts])


def solution(mesh):
    in_specs = (
        P("elem", None, None),
        P("elem", None, None),
        P("elem", None),
        P("elem", None, None),
        P("elem"),
        P("elem", None),
        P("elem", None, None),
    )
    out_specs = P("elem", None)
    return jax.shard_map(body, mesh=mesh, in_specs=in_specs, out_specs=out_specs, check_vma=False)
```
